128 devices in a mesh: ctx: 32 (over z, y, x_lo), wa: 4 (over x_hi, core).
Axes of the slice: x: 4 (x_hi: 2, x_lo: 2; x = x_hi * 2 + x_lo), y: 4, z: 4, core: 2. Of those that a mesh axis runs over, the one named last changes fastest.
Arguments:
- tokens: bfloat16 [8192, 1024], P('ctx'), may hold values from -6 to 6
- cotangent: bfloat16 [8192, 1024], P('ctx'), may hold values from -6 to 6
- pairing: int32 [32], replicated, may hold values from 0 to 31, each once
- routes: int32 [8192, 8], P('ctx'), may hold values from 0 to 15, all different within a row
- norm_attn: float32 [1024], replicated, may hold values from 0.25 to 1.75
- w_query: bfloat16 [1024, 1024], P(None, 'wa'), may hold values from -0.1875 to 0.1875
- w_key: bfloat16 [1024, 512], P(None, 'wa'), may hold values from -0.1875 to 0.1875
- w_value: bfloat16 [1024, 512], P(None, 'wa'), may hold values from -0.1875 to 0.1875
- w_out: bfloat16 [1024, 1024], P('wa'), may hold values from -1.5 to 1.5
- norm_moe: float32 [1024], replicated, may hold values from 0.25 to 1.75
- w_router: bfloat16 [1024, 16], replicated, may hold values from -0.09375 to 0.09375
- w_gate: bfloat16 [16, 1024, 512], P('wa'), may hold values from -0.1875 to 0.1875
- w_up: bfloat16 [16, 1024, 512], P('wa'), may hold values from -0.1875 to 0.1875
- w_down: bfloat16 [16, 512, 1024], P('wa'), may hold values from -0.5 to 0.5
Outputs:
- output: bfloat16 [8192, 1024], P('ctx')
- grad_tokens: bfloat16 [8192, 1024], P('ctx')
- grad_norm_attn: float32 [1024], P('ctx')
- grad_query: float32 [1024, 1024], P('ctx', 'wa')
- grad_key: float32 [1024, 512], P('ctx', 'wa')
- grad_value: float32 [1024, 512], P('ctx', 'wa')
- grad_out: float32 [1024, 1024], P('wa', 'ctx')
- grad_norm_moe: float32 [1024], P('ctx')
- grad_router: float32 [1024, 16], P('ctx')
- grad_gate: float32 [16, 1024, 512], P('wa', 'ctx')
- grad_up: float32 [16, 1024, 512], P('wa', 'ctx')
- grad_down: float32 [16, 512, 1024], P('wa', 'ctx')
The draws below stay inside these ranges and needn't reach their ends.
Inputs may be any that keep to these rules, and one draw needn't show every extreme that they name: `pairing`: a permutation. `routes`: each row names 8 different experts, and every expert is named somewhere.
All inputs are finite; a program needn't handle non-finite values.
Results may differ from the reference program's by a relative error of at most 0.033.
Values may be sent and summed in bfloat16 or wider, within the bound.
No kernel may reach another device: no remote copies, remote signals or barrier semaphores. Data moves between devices by JAX's collectives and lax.ppermute only.
A program may use at most 128 MiB of HBM per device.

```python
import math
import jax
import jax.numpy as jnp
from jax import lax

D = 1024
HEADS = 16
KV_HEADS = 8
HEAD_DIM = 64
FF = 512
TOP = 8
BLOCK = 128
SEQ = 8192
NBLK = 64
EXPERTS = 16


def shard_levels(stream_key, extent, pieces, least, largest):
    factor_of, own = 1.0, jax.random.fold_in(stream_key, 6)
    for dim, blocks in pieces:
        steps = jnp.exp(jax.random.uniform(jax.random.fold_in(own, dim), (blocks,), jnp.float32, least / len(pieces), largest / len(pieces)))
        factor_of = factor_of * jnp.repeat(steps, extent[dim] // blocks).reshape([-1 if axis == dim else 1 for axis in range(len(extent))])
    return factor_of


def distinct(key, rows, count, top, lift):
    ranking = jax.random.permutation(jax.random.fold_in(key, 1), count)
    boost = ranking
    for power in range(3):
        boost = boost * boost // count
    boost = boost * lift // count
    tickets = jax.random.randint(jax.random.fold_in(key, 2), (rows, count), 0, 4096) + boost
    sure = jax.random.permutation(jax.random.fold_in(key, 3), rows)[jnp.arange(count) % rows]
    tickets = jnp.where(jnp.arange(rows)[:, None] == sure[None, :], 1 << 14, tickets)
    merit = tickets * count + jnp.arange(count)
    return lax.top_k(merit.astype(jnp.int32), top)[1].astype(jnp.int32)


def bell_draw(key, extent, deviation, bound, pieces=(), kind=jnp.bfloat16):
    values = deviation * jax.random.normal(key, extent, jnp.float32)
    if pieces:
        values = values * shard_levels(key, extent, pieces, -0.22, 0.18)
    return jnp.clip(values, -bound, bound).astype(kind)


def setup_inputs(seed: int = 0) -> dict:
    key_of = jax.random.split(jax.random.key(seed), 15)
    tokens = bell_draw(key_of[0], (SEQ, D), 1.0, 6.0, ((0, 32),))
    cotangent = bell_draw(key_of[1], (SEQ, D), 1.0, 6.0, ((0, 32),))
    pairing = jax.random.permutation(key_of[2], NBLK // 2).astype(jnp.int32)
    routes = distinct(key_of[3], SEQ, EXPERTS, TOP, 4096)
    norm_attn = jnp.clip(1.0 + 0.15 * jax.random.normal(key_of[4], (D,), jnp.float32), 0.25, 1.75)
    w_query = bell_draw(key_of[5], (D, HEADS * HEAD_DIM), D ** -0.5, 0.1875, ((1, 4),))
    w_key = bell_draw(key_of[6], (D, KV_HEADS * HEAD_DIM), D ** -0.5, 0.1875, ((1, 4),))
    w_value = bell_draw(key_of[7], (D, KV_HEADS * HEAD_DIM), D ** -0.5, 0.1875, ((1, 4),))
    w_out = bell_draw(key_of[8], (HEADS * HEAD_DIM, D), (HEADS * HEAD_DIM // 64) ** -0.5, 1.5, ((0, 4),))
    norm_moe = jnp.clip(1.0 + 0.15 * jax.random.normal(key_of[9], (D,), jnp.float32), 0.25, 1.75)
    w_router = bell_draw(key_of[10], (D, EXPERTS), (4 * D) ** -0.5, 0.09375)
    w_gate = bell_draw(key_of[11], (EXPERTS, D, FF), D ** -0.5, 0.1875, ((0, 4),))
    w_up = bell_draw(key_of[12], (EXPERTS, D, FF), D ** -0.5, 0.1875, ((0, 4),))
    w_down = bell_draw(key_of[13], (EXPERTS, FF, D), (FF // 4) ** -0.5, 0.5, ((0, 4),))
    return dict(tokens=tokens, cotangent=cotangent, pairing=pairing, routes=routes, norm_attn=norm_attn, w_query=w_query, w_key=w_key, w_value=w_value, w_out=w_out, norm_moe=norm_moe, w_router=w_router, w_gate=w_gate, w_up=w_up, w_down=w_down)


@jax.custom_vjp
def low(v):
    return lax.optimization_barrier(v.astype(jnp.bfloat16)).astype(jnp.float32)

@jax.custom_vjp
def low_back(v):
    return v

def low_keep(v):
    return (low(v), None)

def low_pass(kept, grad):
    return (grad,)

def back_keep(v):
    return (v, None)

def back_low(kept, grad):
    return (low(grad),)
low.defvjp(low_keep, low_pass)
low_back.defvjp(back_keep, back_low)
EPS = 1e-05
THETA = 10000.0
HIGH = lax.Precision.HIGHEST

def product(left, right):
    return jnp.dot(left, right, precision=HIGH)

def rms(values, gain):
    return values * lax.rsqrt(lax.optimization_barrier(jnp.mean(values * values, -1, keepdims=True)) + EPS) * gain

def rotate(heads, pos):
    half = heads.shape[-1] // 2
    freq = THETA ** (-(jnp.arange(half, dtype=jnp.float32) * 2.0 / heads.shape[-1]))
    angle = pos.astype(jnp.float32)[:, None] * freq[None, :]
    cosine = jnp.cos(angle)[:, None, :]
    sine = jnp.sin(angle)[:, None, :]
    first = heads[..., :half]
    second = heads[..., half:]
    return jnp.concatenate([first * cosine - second * sine, second * cosine + first * sine], -1)

def positions_of(pairing):
    count = pairing.shape[0]
    starts = jnp.stack([pairing * BLOCK, (2 * count - 1 - pairing) * BLOCK], 1)
    steps = jnp.arange(BLOCK, dtype=jnp.int32)
    return (starts[:, :, None] + steps[None, None, :]).reshape(-1).astype(jnp.int32)

def forward(pos, routes, x, g_attn, wq, wk, wv, wo, g_moe, wr, wg, wu, wd):
    seq = x.shape[0]
    group = HEADS // KV_HEADS
    scale = HEAD_DIM ** (-0.5)
    h1 = low(rms(x, g_attn))
    q = low_back(product(h1, wq)).reshape(seq, HEADS, HEAD_DIM)
    k = low_back(product(h1, wk)).reshape(seq, KV_HEADS, HEAD_DIM)
    v = low(low_back(product(h1, wv))).reshape(seq, KV_HEADS, HEAD_DIM)
    rq = low(rotate(q, pos)).reshape(seq, KV_HEADS, group, HEAD_DIM)
    rk = low(rotate(k, pos))
    span = math.gcd(512, seq)

    def attend(pair):
        qblk, pblk = pair
        s = low_back(jnp.einsum('qkgd,skd->kgqs', qblk, rk, precision=HIGH) * scale)
        s = jnp.where(pos[None, None, None, :] <= pblk[None, None, :, None], s, -1e+30)
        top = lax.optimization_barrier(jnp.max(s, -1, keepdims=True))
        expd = jnp.exp(s - top)
        probs = expd / lax.optimization_barrier(jnp.sum(expd, -1, keepdims=True))
        return jnp.einsum('kgqs,skd->qkgd', low(probs), v, precision=HIGH)
    blocks = lax.map(jax.checkpoint(attend), (rq.reshape(seq // span, span, KV_HEADS, group, HEAD_DIM), pos.reshape(seq // span, span)))
    attn = blocks.reshape(seq, HEADS * HEAD_DIM)
    x2 = x + low_back(product(low(low_back(attn)), wo))
    h2 = low(rms(x2, g_moe))
    logits = low_back(product(h2, wr))
    onehot = (routes[:, :, None] == jnp.arange(EXPERTS, dtype=jnp.int32)[None, None, :]).astype(jnp.float32)
    chosen = lax.optimization_barrier(jnp.sum(logits[:, None, :] * onehot, -1))
    top = lax.optimization_barrier(jnp.max(chosen, -1, keepdims=True))
    expd = jnp.exp(chosen - top)
    gates = expd / lax.optimization_barrier(jnp.sum(expd, -1, keepdims=True))
    mix = lax.optimization_barrier(jnp.sum(gates[:, :, None] * onehot, 1))

    def expert_step(total, params):
        wge, wue, wde, column = params
        ga = low_back(product(h2, wge))
        up = low_back(product(h2, wue))
        hid = low(ga * jax.nn.sigmoid(ga) * up)
        outcome = low_back(product(hid, wde))
        return (total + column[:, None] * outcome, None)
    moe, unused = lax.scan(jax.checkpoint(expert_step), jnp.zeros((seq, D), jnp.float32), (wg, wu, wd, mix.T))
    return x2 + moe

def reference(tokens, cotangent, pairing, routes, norm_attn, w_query, w_key, w_value, w_out, norm_moe, w_router, w_gate, w_up, w_down):
    pos = positions_of(pairing)
    params = tuple((a.astype(jnp.float32) for a in (tokens, norm_attn, w_query, w_key, w_value, w_out, norm_moe, w_router, w_gate, w_up, w_down)))
    out, pull = jax.vjp(lambda *p: forward(pos, routes, *p), *params)
    grads = pull(cotangent.astype(jnp.float32))
    return (out.astype(jnp.bfloat16), grads[0].astype(jnp.bfloat16), grads[1], grads[2], grads[3], grads[4], grads[5], grads[6], grads[7], grads[8], grads[9], grads[10])
```

```python
import jax
import jax.numpy as jnp
from jax import lax
from jax.sharding import Mesh
from jax.sharding import PartitionSpec as P

HEAD_DIM = 64
EPS = 1e-05
THETA = 10000.0
CTX = ("z", "y", "xl")
WA = ("xh", "c")
ZY = ("z", "y")
RING = ("xl", "xh", "c")
BF16 = jnp.bfloat16
F32 = jnp.float32
SWAP = [(0, 1), (1, 0)]


def dot(left, right):
    return jnp.dot(left, right, preferred_element_type=F32)


def outer(left, right):
    return lax.dot_general(left, right, (((0,), (0,)), ((), ())), preferred_element_type=F32)


def inner(left, right):
    return lax.dot_general(left, right, (((1,), (1,)), ((), ())), preferred_element_type=F32)


def rms(values, gain):
    factor = lax.rsqrt(jnp.mean(values * values, -1, keepdims=True) + EPS)
    return values * factor * gain, factor


def norm_back(values, factor, gain, grad):
    scaled = grad * gain
    grad_gain = jnp.sum(grad * values * factor, 0)
    grad_values = factor * scaled - values * factor**3 * jnp.mean(
        scaled * values, -1, keepdims=True
    )
    return grad_values, grad_gain


def angles(pos):
    half = HEAD_DIM // 2
    freq = THETA ** (-(jnp.arange(half, dtype=F32) * 2.0 / HEAD_DIM))
    angle = pos.astype(F32)[:, None] * freq[None, :]
    return jnp.cos(angle), jnp.sin(angle)


def rotate(flat, cosine, sine):
    rows, width = flat.shape
    heads = flat.reshape(rows, width // HEAD_DIM, HEAD_DIM)
    half = HEAD_DIM // 2
    cosine, sine = cosine[:, None, :], sine[:, None, :]
    first, second = heads[..., :half], heads[..., half:]
    return jnp.concatenate(
        [first * cosine - second * sine, second * cosine + first * sine], -1
    ).reshape(rows, width)


def swap_x(mine):
    other = lax.ppermute(mine, "xl", SWAP)
    low = lax.axis_index("xl") == 0
    return jnp.concatenate([jnp.where(low, mine, other), jnp.where(low, other, mine)], 0)


def scores_of(queries, keys, qpos, start, span, scale):
    kpos = start + jnp.arange(span, dtype=jnp.int32)
    raw = jnp.einsum("qgd,sd->gqs", queries, keys, preferred_element_type=F32) * scale
    return jnp.where(kpos[None, None, :] <= qpos[None, :, None], raw, -1e30)


def attend(queries, keys, values, qpos, span, scale, count):
    shape = (queries.shape[1], queries.shape[0])

    def step(index, carry):
        top, summed = carry
        kblk = lax.dynamic_slice_in_dim(keys, index * span, span, 0)
        scores = scores_of(queries, kblk, qpos, index * span, span, scale)
        new_top = jnp.maximum(top, jnp.max(scores, -1))
        summed = summed * jnp.exp(top - new_top) + jnp.sum(jnp.exp(scores - new_top[..., None]), -1)
        return (new_top, summed)

    top, summed = lax.fori_loop(
        0, count, step, (jnp.full(shape, -1e30, F32), jnp.zeros(shape, F32))
    )
    lse = top + jnp.log(summed)

    def step2(index, acc):
        kblk = lax.dynamic_slice_in_dim(keys, index * span, span, 0)
        vblk = lax.dynamic_slice_in_dim(values, index * span, span, 0)
        probs = jnp.exp(
            scores_of(queries, kblk, qpos, index * span, span, scale) - lse[..., None]
        ).astype(BF16)
        return acc + jnp.einsum("gqs,sd->qgd", probs, vblk, preferred_element_type=F32)

    return lax.fori_loop(0, count, step2, jnp.zeros(queries.shape, F32)), lse


def attend_back(queries, keys, values, qpos, lse, grad_o, delta, span, scale, count):
    def step(index, carry):
        grad_q, grad_k, grad_v = carry
        kblk = lax.dynamic_slice_in_dim(keys, index * span, span, 0)
        vblk = lax.dynamic_slice_in_dim(values, index * span, span, 0)
        probs = jnp.exp(scores_of(queries, kblk, qpos, index * span, span, scale) - lse[..., None])
        dprob = jnp.einsum("qgd,sd->gqs", grad_o, vblk, preferred_element_type=F32)
        dscore = (probs * (dprob - delta[..., None])).astype(BF16)
        grad_q = (
            grad_q
            + jnp.einsum("gqs,sd->qgd", dscore, kblk, preferred_element_type=F32) * scale
        )
        kpart = jnp.einsum("gqs,qgd->sd", dscore, queries, preferred_element_type=F32) * scale
        vpart = jnp.einsum("gqs,qgd->sd", probs.astype(BF16), grad_o, preferred_element_type=F32)
        grad_k = lax.dynamic_update_slice_in_dim(grad_k, kpart, index * span, 0)
        grad_v = lax.dynamic_update_slice_in_dim(grad_v, vpart, index * span, 0)
        return (grad_q, grad_k, grad_v)

    start = (
        jnp.zeros(queries.shape, F32),
        jnp.zeros(keys.shape, F32),
        jnp.zeros(values.shape, F32),
    )
    return lax.fori_loop(0, count, step, start)


def on_device(
    tokens,
    cotangent,
    pairing,
    routes,
    norm_attn,
    w_query,
    w_key,
    w_value,
    w_out,
    norm_moe,
    w_router,
    w_gate,
    w_up,
    w_down,
):
    zy = lax.axis_index(ZY)
    xl = lax.axis_index("xl")
    wa = lax.axis_index(WA)
    rows, width = tokens.shape
    block = rows // 2
    both = 2 * rows
    count_ctx = pairing.shape[0]
    blocks = 2 * count_ctx
    groups = count_ctx // 2
    total = blocks * block
    scale = HEAD_DIM ** (-0.5)
    hq = w_query.shape[1] // 2
    hk = w_key.shape[1] // 2
    hall = hq + 2 * hk

    w_out_all = lax.all_gather(w_out, WA, axis=0, tiled=True)
    w_in = jnp.concatenate(
        [
            w[:, half * n : (half + 1) * n]
            for half in (0, 1)
            for w, n in ((w_query, hq), (w_key, hk), (w_value, hk))
        ],
        1,
    )
    w_in_all = lax.all_gather(w_in, WA, axis=0, tiled=False)

    pair = lax.dynamic_slice_in_dim(pairing, zy * 2, 2)
    starts = jnp.stack([pair, blocks - 1 - pair], 1).reshape(4) * block
    qpos = (starts[:, None] + jnp.arange(block, dtype=jnp.int32)[None, :]).reshape(both)
    own_pos = lax.dynamic_slice_in_dim(qpos, xl * rows, rows)

    xf_own = tokens.astype(F32)
    normed1, factor1 = rms(xf_own, norm_attn)
    h1_own = normed1.astype(BF16)
    cosine, sine = angles(own_pos)
    query = rotate(dot(h1_own, w_query), cosine, sine).astype(BF16)
    key = rotate(dot(h1_own, w_key), cosine, sine).astype(BF16)
    value = dot(h1_own, w_value).astype(BF16)
    halves = jnp.stack(
        [
            jnp.concatenate(
                [a[:, half * n : (half + 1) * n] for a, n in ((query, hq), (key, hk), (value, hk))], 1
            )
            for half in (0, 1)
        ]
    )
    keep = lax.dynamic_index_in_dim(halves, xl, 0, False)
    give = lax.dynamic_index_in_dim(halves, 1 - xl, 0, False)
    got = lax.ppermute(give, "xl", SWAP)
    low = xl == 0
    qkv = jnp.concatenate([jnp.where(low, keep, got), jnp.where(low, got, keep)], 0)
    rq = qkv[:, :hq]
    kv_mine = qkv[:, hq:]

    kv_all = lax.all_to_all(
        jnp.broadcast_to(kv_mine[None], (groups,) + kv_mine.shape), ZY, 0, 0, tiled=False
    ).reshape(blocks, block, 2 * hk)

    x_pair = swap_x(tokens)
    dy_pair = swap_x(cotangent)
    routes_pair = swap_x(routes.astype(F32)).astype(jnp.int32)

    ranks = jnp.arange(count_ctx, dtype=jnp.int32)
    inverse = jnp.sum(jnp.where(pairing[None, :] == ranks[:, None], ranks[None, :], 0), 1)
    slot = jnp.concatenate([inverse * 2, inverse[::-1] * 2 + 1])
    sorted_kv = kv_all[slot].reshape(total, 2 * hk)
    keys, values = sorted_kv[:, :hk], sorted_kv[:, hk:]
    span = 512
    count = jnp.max(qpos) // span + 1
    q3 = rq.reshape(both, 2, HEAD_DIM)
    attn, lse = attend(q3, keys, values, qpos, span, scale, count)
    attn_low = attn.reshape(both, hq).astype(BF16)

    o_all = lax.all_to_all(
        jnp.broadcast_to(attn_low[None], (8,) + attn_low.shape), RING, 0, 0, tiled=False
    )
    w_out_ring = w_out_all.reshape(4, 2, hq, width).transpose(1, 0, 2, 3).reshape(8 * hq, width)
    o_cat = jnp.transpose(o_all, (1, 0, 2)).reshape(both, 8 * hq)
    xf = x_pair.astype(F32)
    x2 = xf + dot(o_cat, w_out_ring)
    normed2, factor2 = rms(x2, norm_moe)
    h2 = normed2.astype(BF16)
    experts_all = w_router.shape[1]
    logits = dot(h2, w_router)
    used = jnp.any(
        routes_pair[:, :, None] == jnp.arange(experts_all, dtype=jnp.int32)[None, None, :], 1
    )
    masked = jnp.where(used, logits, -jnp.inf)
    expd = jnp.where(used, jnp.exp(logits - jnp.max(masked, -1, keepdims=True)), 0.0)
    mix_all = expd / jnp.sum(expd, -1, keepdims=True)

    local = w_gate.shape[0] // 2
    first = wa * 2 * local + xl * local
    mix = lax.dynamic_slice_in_dim(mix_all, first, local, 1)
    wg = lax.dynamic_slice_in_dim(w_gate, xl * local, local, 0)
    wu = lax.dynamic_slice_in_dim(w_up, xl * local, local, 0)
    wd = lax.dynamic_slice_in_dim(w_down, xl * local, local, 0)
    dyf = dy_pair.astype(F32)
    moe = jnp.zeros((both, width), F32)
    dh2_part = jnp.zeros((both, width), F32)
    dmix_cols = []
    grads = []
    for e in range(local):
        ga = dot(h2, wg[e])
        up = dot(h2, wu[e])
        sig = jax.nn.sigmoid(ga)
        act = ga * sig
        hid = (act * up).astype(BF16)
        eo = dot(hid, wd[e])
        gate = mix[:, e : e + 1]
        moe = moe + gate * eo
        dmix_cols.append(jnp.sum(dyf * eo, -1))
        deo = (gate * dyf).astype(BF16)
        dhid = inner(deo, wd[e])
        dga = (dhid * up * (sig * (1.0 + ga * (1.0 - sig)))).astype(BF16)
        dup = (dhid * act).astype(BF16)
        dh2_part = dh2_part + inner(dga, wg[e]) + inner(dup, wu[e])
        grads.append((outer(h2, dga), outer(h2, dup), outer(hid, deo)))

    def expert_slot(col):
        return jnp.where(
            jnp.arange(128, dtype=jnp.int32)[None, :] == first + col, dmix_cols[col][:, None], 0.0
        )

    part = jnp.concatenate(
        [dh2_part, moe, sum(expert_slot(e) for e in range(local))], 1
    ).astype(BF16)
    part = lax.all_to_all(part.reshape(8, both // 8, 2 * width + 128), RING, 0, 0, tiled=False)
    part = jnp.sum(part.astype(F32), 0)

    def spread(grad):
        return grad.astype(BF16)

    packed = jnp.stack(
        [
            jnp.concatenate(
                [
                    jnp.stack([g[0] for g in grads]).astype(BF16).reshape(local, groups, -1, 512).transpose(1, 0, 2, 3).reshape(groups, -1, 512),
                    jnp.stack([g[1] for g in grads]).astype(BF16).reshape(local, groups, -1, 512).transpose(1, 0, 2, 3).reshape(groups, -1, 512),
                    jnp.stack([g[2] for g in grads]).astype(BF16).reshape(local, groups, -1, 1024).transpose(1, 0, 2, 3).reshape(groups, -1, 512),
                ],
                1,
            )
        ]
    )[0]
    reduced = lax.psum_scatter(packed, "z", scatter_dimension=0, tiled=True)
    reduced = lax.psum_scatter(reduced, "y", scatter_dimension=0, tiled=True)[0]

    few = both // 8
    lo_row = (xl * 4 + wa) * few
    dh2_e = part[:, :width]
    moe_rows = part[:, width : 2 * width]
    dmix_rows = part[:, 2 * width : 2 * width + experts_all]
    mine = lambda a: lax.dynamic_slice_in_dim(a, lo_row, few, 0)
    x2_rows, factor2_rows, mix_rows, dy_rows = mine(x2), mine(factor2), mine(mix_all), mine(dyf)
    out_rows = (x2_rows + moe_rows).astype(BF16)
    output = lax.all_gather(out_rows, WA, axis=0, tiled=True)
    dlogits = (
        mix_rows * (dmix_rows - jnp.sum(mix_rows * dmix_rows, -1, keepdims=True))
    ).astype(BF16)
    dh2 = dh2_e + inner(dlogits, w_router)
    dx2_norm, gnm_part = norm_back(x2_rows, factor2_rows, norm_moe, dh2)
    dx2_rows = (dy_rows + dx2_norm).astype(BF16)
    extra = jnp.concatenate(
        [dlogits, gnm_part.astype(BF16).reshape(few, width // few), jnp.zeros((few, 96), BF16)], 1
    )
    payload = jnp.concatenate([dx2_rows, extra], 1)
    full = lax.all_to_all(
        jnp.broadcast_to(payload[None], (8,) + payload.shape), RING, 0, 0, tiled=False
    )
    da = full[:, :, :width].reshape(both, width)
    dlogits_pair = full[:, :, width : width + experts_all].reshape(both, experts_all)
    gnm_all = full[:, :, width + experts_all : width + experts_all + width // few].astype(F32).reshape(8, width)
    own_four = (jnp.arange(8, dtype=jnp.int32) // 4 == xl)[:, None]
    gnm_own = jnp.sum(jnp.where(own_four, gnm_all, 0.0), 0)

    w_out_half = lax.dynamic_slice_in_dim(w_out, xl * hq, hq, 0)
    grad_o = inner(da, w_out_half).astype(BF16).reshape(both, 2, HEAD_DIM)
    delta = jnp.transpose(jnp.sum(grad_o.astype(F32) * attn, -1), (1, 0))
    grad_q, grad_k, grad_v = attend_back(
        q3, keys, values, qpos, lse, grad_o, delta, span, scale, count
    )
    grad_kv = jnp.concatenate([grad_k, grad_v], 1).astype(BF16).reshape(blocks, block, 2 * hk)
    order = jnp.stack([pairing, blocks - 1 - pairing], 1).reshape(blocks)
    grad_kv = lax.all_to_all(
        grad_kv[order].reshape(groups, both, 2 * hk), ZY, 0, 0, tiled=False
    )
    grad_kv = jnp.sum(grad_kv.astype(F32), 0)
    cos2, sin2 = angles(qpos)
    dq = rotate(grad_q.reshape(both, hq), cos2, -sin2).astype(BF16)
    dk = rotate(grad_kv[:, :hk], cos2, -sin2).astype(BF16)
    dv = grad_kv[:, hk:].astype(BF16)
    dqkv = jnp.concatenate([dq, dk, dv], 1)

    h1 = rms(xf, norm_attn)[0].astype(BF16)
    dqkv_all = lax.all_to_all(
        jnp.broadcast_to(dqkv.reshape(2, 1, rows, hall), (2, 4, rows, hall)).reshape(8, rows, hall),
        RING,
        0,
        0,
        tiled=False,
    )
    dh1 = jnp.zeros((rows, width), F32)
    for half in (0, 1):
        for r in range(4):
            dh1 = dh1 + inner(
                dqkv_all[half * 4 + r], w_in_all[r][:, half * hall : (half + 1) * hall]
            )
    dx_norm, gna_own = norm_back(xf_own, factor1, norm_attn, dh1)
    da_own = lax.dynamic_slice_in_dim(da, xl * rows, rows, 0).astype(F32)
    grad_tokens = (da_own + dx_norm).astype(BF16)

    h2_own = lax.dynamic_slice_in_dim(h2, xl * rows, rows, 0)
    dlogits_own = lax.dynamic_slice_in_dim(dlogits_pair, xl * rows, rows, 0)
    grad_router = outer(h2_own, dlogits_own)
    small = jnp.concatenate(
        [
            outer(h1, dqkv),
            outer(da, attn_low),
            grad_router,
            gnm_own[:, None],
            gna_own[:, None],
            jnp.zeros((width, 128 - experts_all - 2), F32),
        ],
        1,
    ).astype(BF16)
    small = lax.all_to_all(small.reshape(count_ctx, -1, small.shape[1]), CTX, 0, 0, tiled=False)
    small = jnp.sum(small.reshape(groups, 2, -1, small.shape[2]).astype(F32), 0)
    grad_query = jnp.concatenate([small[0, :, :hq], small[1, :, :hq]], 1)
    grad_key = jnp.concatenate([small[0, :, hq : hq + hk], small[1, :, hq : hq + hk]], 1)
    grad_value = jnp.concatenate([small[0, :, hq + hk : hall], small[1, :, hq + hk : hall]], 1)
    grad_out = jnp.concatenate(
        [small[0, :, hall : hall + hq].T, small[1, :, hall : hall + hq].T], 0
    )
    rest = small[0, :, hall + hq :] + small[1, :, hall + hq :]
    grad_router = rest[:, :experts_all]
    grad_norm_moe = rest[:, experts_all]
    grad_norm_attn = rest[:, experts_all + 1]

    nrow = width // groups
    drow = 512 // groups
    gate_up = reduced[: 4 * nrow].reshape(2, local, 2, nrow // 2, 512)
    down = reduced[4 * nrow :].reshape(1, local, 2, drow // 2, 1024).reshape(1, local, 2, drow, 512)
    by_dest = jnp.concatenate([gate_up.transpose(2, 0, 1, 3, 4).reshape(2, -1, 512), down.transpose(2, 0, 1, 3, 4).reshape(2, -1, 512)], 1)
    keep_w = lax.dynamic_index_in_dim(by_dest, xl, 0, False)
    got_w = lax.ppermute(lax.dynamic_index_in_dim(by_dest, 1 - xl, 0, False), "xl", SWAP)
    pairw = jnp.stack([jnp.where(low, keep_w, got_w), jnp.where(low, got_w, keep_w)]).astype(F32)
    half_n = nrow // 2
    n1 = local * half_n
    grad_gate = pairw[:, :n1].reshape(2 * local, half_n, 512)
    grad_up = pairw[:, n1 : 2 * n1].reshape(2 * local, half_n, 512)
    grad_down = pairw[:, 2 * n1 :].reshape(2 * local, drow // 2, 1024)
    return (
        output,
        grad_tokens,
        grad_norm_attn,
        grad_query,
        grad_key,
        grad_value,
        grad_out,
        grad_norm_moe,
        grad_router,
        grad_gate,
        grad_up,
        grad_down,
    )


def solution(mesh):
    fine = Mesh(mesh.devices.reshape(4, 4, 2, 2, 2), ("z", "y", "xl", "xh", "c"))
    return jax.shard_map(
        on_device,
        mesh=fine,
        in_specs=(
            P(CTX, None),
            P(CTX, None),
            P(),
            P(CTX, None),
            P(),
            P(None, WA),
            P(None, WA),
            P(None, WA),
            P(WA, None),
            P(),
            P(),
            P(WA, None, None),
            P(WA, None, None),
            P(WA, None, None),
        ),
        out_specs=(
            P(CTX, None),
            P(CTX, None),
            P(CTX),
            P(CTX, WA),
            P(CTX, WA),
            P(CTX, WA),
            P(WA, CTX),
            P(CTX),
            P(CTX, None),
            P(WA, CTX, None),
            P(WA, CTX, None),
            P(WA, CTX, None),
        ),
        check_vma=False,
    )
```

```python
import jax
import jax.numpy as jnp
from jax import lax
from jax.experimental import pallas as pl
from jax.experimental.pallas import tpu as pltpu
from jax.sharding import Mesh
from jax.sharding import PartitionSpec as P

HEAD_DIM = 64
EPS = 1e-05
THETA = 10000.0
CTX = ("z", "y", "xl")
WA = ("xh", "c")
ZY = ("z", "y")
CHIPS = ("xl", "xh")
BF16 = jnp.bfloat16
F32 = jnp.float32
SWAP = [(0, 1), (1, 0)]


def dot(left, right):
    return jnp.dot(left, right, preferred_element_type=F32)


def outer(left, right):
    return lax.dot_general(left, right, (((0,), (0,)), ((), ())), preferred_element_type=F32)


def inner(left, right):
    return lax.dot_general(left, right, (((1,), (1,)), ((), ())), preferred_element_type=F32)


def rms(values, gain):
    factor = lax.rsqrt(jnp.mean(values * values, -1, keepdims=True) + EPS)
    return values * factor * gain, factor


def swap_x(mine):
    other = lax.ppermute(mine, "xl", SWAP)
    low = lax.axis_index("xl") == 0
    return jnp.concatenate([jnp.where(low, mine, other), jnp.where(low, other, mine)], 0)


TILE = 512
LIMIT = 48 * 1024 * 1024


def full_turn(flat, cosine, sine):
    rows, width = flat.shape
    lane = lax.broadcasted_iota(jnp.int32, (rows, 128), 1)
    first = (lane & 63) < 32
    parts = []
    for n in range(width // 128):
        piece = flat[:, n * 128 : (n + 1) * 128]
        other = jnp.where(first, pltpu.roll(piece, 96, 1), pltpu.roll(piece, 32, 1))
        parts.append(piece * cosine + other * sine)
    return parts[0] if len(parts) == 1 else jnp.concatenate(parts, 1)


def lane_angles(pos):
    lane = jnp.arange(128, dtype=jnp.int32)
    freq = THETA ** (-((lane % 32).astype(F32) * 2.0 / HEAD_DIM))
    angle = pos.astype(F32)[:, None] * freq[None, :]
    sign = jnp.where(lane % 64 < 32, -1.0, 1.0)
    return jnp.cos(angle), jnp.sin(angle) * sign[None, :]


def heads_across(block, low):
    turned = block.T
    both = jnp.concatenate([turned[:64], turned[64:]], 1)
    zero = jnp.zeros_like(both)
    return jnp.concatenate([both, zero] if low == 0 else [zero, both], 0)


def heads_back(both):
    return jnp.concatenate([both[:, :128], both[:, 128:]], 0).T


def attend_kernel(place, slot, q_ref, kv_ref, low_ref, o_ref, lse_ref, ks_ref, kt_ref):
    per = TILE // 128

    def sort(tile, unused):
        for j in range(per):
            block = kv_ref[slot[tile * per + j]]
            ks_ref[tile, j * 128 : (j + 1) * 128, :] = block
            kt_ref[tile, :, j * 128 : (j + 1) * 128] = block.astype(F32).T.astype(BF16)
        return unused

    lax.fori_loop(0, ks_ref.shape[0], sort, 0)
    apart = lax.broadcasted_iota(jnp.int32, (TILE, 256), 0) - (
        lax.broadcasted_iota(jnp.int32, (TILE, 256), 1) & 127
    )
    for b in range(q_ref.shape[0] // 128):
        own = place[b]
        query = q_ref[b * 128 : (b + 1) * 128, :].astype(F32) * HEAD_DIM**-0.5
        query = heads_across(query, 0).astype(BF16)
        last = own // per

        def step(tile, carry, masked):
            top, summed, acc = carry
            scores = dot(ks_ref[tile], query)
            if masked:
                scores = jnp.where(apart <= own * 128 - tile * TILE, scores, -1e30)
            new_top = jnp.maximum(top, jnp.max(scores, 0, keepdims=True))
            keep = jnp.exp(top - new_top)
            probs = jnp.exp(scores - new_top)
            summed = summed * keep + jnp.sum(probs, 0, keepdims=True)
            acc = acc * keep + dot(kt_ref[tile], probs.astype(BF16))
            return new_top, summed, acc

        carry = (
            jnp.full((1, 256), -1e30, F32),
            jnp.zeros((1, 256), F32),
            jnp.zeros((128, 256), F32),
        )
        carry = lax.fori_loop(0, last, lambda tile, c: step(tile, c, False), carry)
        top, summed, acc = step(last, carry, True)
        result = acc[64:] / summed
        o_ref[b] = result
        lse_ref[b] = top + jnp.log(summed)
        low_ref[b * 128 : (b + 1) * 128, :] = heads_back(result).astype(BF16)


def attend(place, slot, rq, kv_all):
    count = rq.shape[0] // 128
    tiles = kv_all.shape[0] * 128 // TILE
    return pl.pallas_call(
        attend_kernel,
        grid_spec=pltpu.PrefetchScalarGridSpec(
            num_scalar_prefetch=2,
            grid=(1,),
            in_specs=[
                pl.BlockSpec(rq.shape, lambda i, *_: (0, 0)),
                pl.BlockSpec(kv_all.shape, lambda i, *_: (0, 0, 0)),
            ],
            out_specs=[
                pl.BlockSpec(rq.shape, lambda i, *_: (0, 0)),
                pl.BlockSpec((count, 64, 256), lambda i, *_: (0, 0, 0)),
                pl.BlockSpec((count, 1, 256), lambda i, *_: (0, 0, 0)),
                pl.BlockSpec((tiles, TILE, 128), lambda i, *_: (0, 0, 0)),
                pl.BlockSpec((tiles, 128, TILE), lambda i, *_: (0, 0, 0)),
            ],
        ),
        out_shape=[
            jax.ShapeDtypeStruct(rq.shape, BF16),
            jax.ShapeDtypeStruct((count, 64, 256), F32),
            jax.ShapeDtypeStruct((count, 1, 256), F32),
            jax.ShapeDtypeStruct((tiles, TILE, 128), BF16),
            jax.ShapeDtypeStruct((tiles, 128, TILE), BF16),
        ],
        compiler_params=pltpu.CompilerParams(vmem_limit_bytes=LIMIT),
        cost_estimate=pl.CostEstimate(
            flops=20_000_000_000, bytes_accessed=8_000_000, transcendentals=4_000_000
        ),
        name="attend",
    )(place, slot, rq, kv_all)


def attend_back_kernel(
    place, slot, me, q_ref, full_ref, other_ref, o_ref, lse_ref, ks_ref, kt_ref, cos_ref, sin_ref, wo_ref,
    dq_ref, dkv_ref, da_ref, rest_ref, acc_ref,
):
    per = TILE // 128

    def clear(tile, unused):
        acc_ref[tile] = jnp.zeros((TILE, 128), F32)
        return unused

    lax.fori_loop(0, acc_ref.shape[0], clear, 0)
    few, width = full_ref.shape[1], da_ref.shape[1]
    for b in range(full_ref.shape[0]):
        for ref, side in ((full_ref, me[2]), (other_ref, 1 - me[2])):
            at = pl.ds(pl.multiple_of(b * 2 * few + side * few, few), few)
            da_ref[at, :] = ref[b, :, :width]
            rest_ref[at, :] = ref[b, :, width:]
    apart = lax.broadcasted_iota(jnp.int32, (TILE, 256), 0) - (
        lax.broadcasted_iota(jnp.int32, (TILE, 256), 1) & 127
    )
    for b in range(q_ref.shape[0] // 128):
        own = place[b]
        sl = slice(b * 128, (b + 1) * 128)
        query = heads_across(q_ref[sl, :].astype(F32) * HEAD_DIM**-0.5, 0)
        grad = inner(da_ref[sl, :], wo_ref[...]).astype(BF16)
        grad = heads_across(grad.astype(F32), 64)
        delta = jnp.sum(grad[64:] * o_ref[b], 0, keepdims=True)
        lse = lse_ref[b]
        right = jnp.concatenate([query, grad], 1).astype(BF16)
        under = jnp.concatenate([query.T, grad.T], 0).astype(BF16)
        last = own // per

        def step(tile, acc, masked):
            prod = dot(ks_ref[tile], right)
            probs = jnp.exp(prod[:, :256] - lse)
            if masked:
                probs = jnp.where(apart <= own * 128 - tile * TILE, probs, 0.0)
            dscore = (probs * (prod[:, 256:] - delta)).astype(BF16)
            acc_ref[tile] += dot(jnp.concatenate([dscore, probs.astype(BF16)], 1), under)
            return acc + dot(kt_ref[tile], dscore)

        acc = lax.fori_loop(
            0, last, lambda tile, c: step(tile, c, False), jnp.zeros((128, 256), F32)
        )
        acc = step(last, acc, True)
        dq = heads_back(acc[:64]) * HEAD_DIM**-0.5
        dq_ref[sl, :] = full_turn(dq, cos_ref[sl, :], -sin_ref[sl, :]).astype(BF16)

    def unsort(tile, unused):
        for j in range(per):
            dkv_ref[slot[tile * per + j]] = acc_ref[tile, j * 128 : (j + 1) * 128, :].astype(BF16)
        return unused

    lax.fori_loop(0, acc_ref.shape[0], unsort, 0)


def attend_back(place, slot, me, rq, full, other, o, lse, ks, kt, cosine, sine, w_out):
    rows = rq.shape[0]
    width = w_out.shape[1]
    blocks = slot.shape[0]
    args = (rq, full, other, o, lse, ks, kt, cosine, sine)
    shapes = [
        jax.ShapeDtypeStruct(rq.shape, BF16),
        jax.ShapeDtypeStruct((blocks, 128, 128), BF16),
        jax.ShapeDtypeStruct((rows, width), BF16),
        jax.ShapeDtypeStruct((rows, 128), BF16),
    ]
    return pl.pallas_call(
        attend_back_kernel,
        grid_spec=pltpu.PrefetchScalarGridSpec(
            num_scalar_prefetch=3,
            grid=(1,),
            in_specs=[whole(a) for a in args]
            + [pl.BlockSpec((rq.shape[1], width), lambda i, place, slot, me: (me[0], 0))],
            out_specs=[whole(a) for a in shapes],
            scratch_shapes=[pltpu.VMEM(ks.shape, F32)],
        ),
        out_shape=shapes,
        compiler_params=pltpu.CompilerParams(vmem_limit_bytes=LIMIT),
        cost_estimate=pl.CostEstimate(
            flops=30_000_000_000, bytes_accessed=8_000_000, transcendentals=4_000_000
        ),
        name="attend_back",
    )(place, slot, me, *args, w_out)


def whole(a):
    rank = len(a.shape)
    return pl.BlockSpec(a.shape, lambda i, *_: (0,) * rank, pipeline_mode=pl.Buffered(1))


def experts_kernel(
    me, o_ref, p_ref, x_ref, dy_ref, routes_ref, wo0, wo1, wo2, wo3, gain_ref, wr_ref,
    wg_ref, wu_ref, wd_ref,
    x2_ref, h2_ref, mix_ref, keep_ref, give_ref, mkeep_ref, mgive_ref, grad_ref,
    dh2_acc, moe_acc, dmix_acc,
):
    step = pl.program_id(0)
    xh, core, first = me[1], me[2], me[3]
    rows = x_ref.shape[0]
    lane = lax.broadcasted_iota(jnp.int32, (rows, 128), 1)

    @pl.when(step == 0)
    def _():
        def heads(ref, side):
            return jnp.concatenate([ref[side], ref[2 + side]], 1)

        near = dot(heads(o_ref, xh), wo0[...]) + dot(heads(p_ref, xh), wo1[...])
        far = dot(heads(o_ref, 1 - xh), wo2[...]) + dot(heads(p_ref, 1 - xh), wo3[...])
        x2 = x_ref[...].astype(F32) + (near + far)
        x2_ref[...] = x2
        h2 = rms(x2, gain_ref[...])[0].astype(BF16)
        h2_ref[...] = h2
        logits = dot(h2, wr_ref[...])
        routes = routes_ref[...]
        used = lane == routes[:, 0:1]
        for k in range(1, routes.shape[1]):
            used = jnp.logical_or(used, lane == routes[:, k : k + 1])
        top = jnp.max(jnp.where(used, logits, -jnp.inf), 1, keepdims=True)
        expd = jnp.where(used, jnp.exp(logits - top), 0.0)
        mix_ref[...] = expd / jnp.sum(expd, 1, keepdims=True)
        dh2_acc[...] = jnp.zeros_like(dh2_acc)
        moe_acc[...] = jnp.zeros_like(moe_acc)
        dmix_acc[...] = jnp.zeros_like(dmix_acc)

    here = lane == first + step
    gate = jnp.sum(jnp.where(here, mix_ref[...], 0.0), 1, keepdims=True)
    h2 = h2_ref[...]
    dy = dy_ref[...].astype(F32)
    ga = dot(h2, wg_ref[0])
    up = dot(h2, wu_ref[0])
    sig = jax.nn.sigmoid(ga)
    act = ga * sig
    hid = (act * up).astype(BF16)
    eo = dot(hid, wd_ref[0])
    moe_acc[...] += gate * eo
    dmix_acc[...] += jnp.where(here, jnp.sum(dy * eo, 1, keepdims=True), 0.0)
    deo = (gate * dy).astype(BF16)
    dhid = inner(deo, wd_ref[0])
    dga = (dhid * up * (sig * (1.0 + ga * (1.0 - sig)))).astype(BF16)
    dup = (dhid * act).astype(BF16)
    dh2_acc[...] += inner(dga, wg_ref[0]) + inner(dup, wu_ref[0])
    groups = grad_ref.shape[0]
    across = grad_ref.shape[2] * 2 // 3
    width = h2.shape[1]
    grad_ref[:, 0, :across, :512] = outer(h2, dga).astype(BF16).reshape(groups, across, 512)
    grad_ref[:, 0, :across, 512:] = outer(h2, dup).astype(BF16).reshape(groups, across, 512)
    grad_ref[:, 0, across:, :] = outer(hid, deo).astype(BF16).reshape(groups, across // 2, width)

    @pl.when(step == pl.num_programs(0) - 1)
    def _():
        few = rows // 8
        for j in range(4):
            for side, out, mout in ((core, keep_ref, mkeep_ref), (1 - core, give_ref, mgive_ref)):
                at = pl.ds(pl.multiple_of((j * 2 + side) * few, few), few)
                out[j, :, :width] = dh2_acc[at, :].astype(BF16)
                out[j, :, width:] = dmix_acc[at, :].astype(BF16)
                mout[j] = moe_acc[at, :].astype(BF16)


def experts(me, o_mine, o_other, x_pair, dy_pair, routes, wo, gain, router, wg, wu, wd, groups):
    rows, width = x_pair.shape
    few = rows // 8
    local = wg.shape[0] // 2
    ff = wg.shape[2]
    args = (o_mine, o_other, x_pair, dy_pair, routes, *wo, gain, router)
    across = width // groups
    shapes = [
        jax.ShapeDtypeStruct((rows, width), F32),
        jax.ShapeDtypeStruct((rows, width), BF16),
        jax.ShapeDtypeStruct((rows, 128), F32),
        jax.ShapeDtypeStruct((4, few, width + 128), BF16),
        jax.ShapeDtypeStruct((4, few, width + 128), BF16),
        jax.ShapeDtypeStruct((4, few, width), BF16),
        jax.ShapeDtypeStruct((4, few, width), BF16),
    ]
    pick = lambda i, me: (me[0] * local + i, 0, 0)
    return pl.pallas_call(
        experts_kernel,
        grid_spec=pltpu.PrefetchScalarGridSpec(
            num_scalar_prefetch=1,
            grid=(local,),
            in_specs=[whole(a) for a in args]
            + [
                pl.BlockSpec((1, width, ff), pick),
                pl.BlockSpec((1, width, ff), pick),
                pl.BlockSpec((1, ff, width), pick),
            ],
            out_specs=[whole(a) for a in shapes]
            + [pl.BlockSpec((groups, 1, across * 3 // 2, width), lambda i, me: (0, i, 0, 0))],
            scratch_shapes=[
                pltpu.VMEM((rows, width), F32),
                pltpu.VMEM((rows, width), F32),
                pltpu.VMEM((rows, 128), F32),
            ],
        ),
        out_shape=shapes
        + [jax.ShapeDtypeStruct((groups, local, across * 3 // 2, width), BF16)],
        compiler_params=pltpu.CompilerParams(vmem_limit_bytes=56 * 1024 * 1024),
        cost_estimate=pl.CostEstimate(
            flops=20_000_000_000, bytes_accessed=20_000_000, transcendentals=1_000_000
        ),
        name="experts",
    )(me, *args, wg, wu, wd)


def start_kernel(me, x_ref, gain_ref, wq_ref, wk_ref, wv_ref, cos_ref, sin_ref, keep_ref, give_ref):
    h1 = rms(x_ref[...].astype(F32), gain_ref[...])[0].astype(BF16)
    cosine, sine = cos_ref[...], sin_ref[...]
    query = full_turn(dot(h1, wq_ref[...]), cosine, sine)
    key = full_turn(dot(h1, wk_ref[...]), cosine, sine)
    value = dot(h1, wv_ref[...])
    left = lax.broadcasted_iota(jnp.int32, key.shape, 1) < 64
    halves = [
        jnp.concatenate([query[:, :128], jnp.where(left, key, pltpu.roll(value, 64, 1))], 1),
        jnp.concatenate([query[:, 128:], jnp.where(left, pltpu.roll(key, 64, 1), value)], 1),
    ]
    low = me[0] == 0
    keep_ref[...] = jnp.where(low, halves[0], halves[1]).astype(BF16)
    give_ref[...] = jnp.where(low, halves[1], halves[0]).astype(BF16)


def start(me, tokens, gain, wq, wk, wv, cosine, sine):
    args = (tokens, gain, wq, wk, wv, cosine, sine)
    shapes = [jax.ShapeDtypeStruct((tokens.shape[0], 256), BF16)] * 2
    return pl.pallas_call(
        start_kernel,
        grid_spec=pltpu.PrefetchScalarGridSpec(
            num_scalar_prefetch=1,
            grid=(1,),
            in_specs=[whole(a) for a in args],
            out_specs=[whole(a) for a in shapes],
        ),
        out_shape=shapes,
        compiler_params=pltpu.CompilerParams(vmem_limit_bytes=LIMIT),
        name="start",
    )(me, *args)


def middle_kernel(me, part_ref, x2_ref, mix_ref, dy_ref, gain_ref, wr_ref, out_ref):
    part = part_ref[0].astype(F32)
    for j in range(1, part_ref.shape[0]):
        part = part + part_ref[j].astype(F32)
    width = x2_ref.shape[1]
    mix, dmix = mix_ref[...], part[:, width:]
    dlogits = (mix * (dmix - jnp.sum(mix * dmix, 1, keepdims=True))).astype(BF16)
    dh2 = part[:, :width] + inner(dlogits, wr_ref[...])
    x2 = x2_ref[...]
    factor = lax.rsqrt(jnp.mean(x2 * x2, -1, keepdims=True) + EPS)
    scaled = dh2 * gain_ref[...]
    dx2 = dy_ref[...].astype(F32) + (
        factor * scaled - x2 * factor**3 * jnp.mean(scaled * x2, -1, keepdims=True)
    )
    gain = jnp.sum(dh2 * x2 * factor, 0, keepdims=True).astype(BF16).astype(F32)
    rows = x2.shape[0]
    per = width // rows
    at = lax.broadcasted_iota(jnp.int32, (rows, width), 1)
    spread = jnp.where(at // per == lax.broadcasted_iota(jnp.int32, (rows, width), 0), gain, 0.0)
    lane = lax.broadcasted_iota(jnp.int32, (width, 128), 1)
    place = lane == lax.broadcasted_iota(jnp.int32, (width, 128), 0) % per + 16
    extra = dot(spread.astype(BF16), place.astype(F32).astype(BF16)) + dlogits.astype(F32)
    for j in range(out_ref.shape[0]):
        out_ref[j, :, :width] = dx2.astype(BF16)
        out_ref[j, :, width:] = extra.astype(BF16)


def middle(me, part, x2, mix, dy, gain, router):
    few = part.shape[1]
    width = x2.shape[1]
    mine = lambda i, me: (me[4], 0)
    shape = jax.ShapeDtypeStruct(part.shape, BF16)
    return pl.pallas_call(
        middle_kernel,
        grid_spec=pltpu.PrefetchScalarGridSpec(
            num_scalar_prefetch=1,
            grid=(1,),
            in_specs=[
                whole(part),
                pl.BlockSpec((few, width), mine),
                pl.BlockSpec((few, 128), mine),
                pl.BlockSpec((few, width), mine),
                whole(gain),
                whole(router),
            ],
            out_specs=whole(shape),
        ),
        out_shape=shape,
        compiler_params=pltpu.CompilerParams(vmem_limit_bytes=LIMIT),
        name="middle",
    )(me, part, x2, mix, dy, gain, router)


def collect_kernel(part_ref, cos_ref, sin_ref, out_ref):
    total = part_ref[0].astype(F32)
    for j in range(1, part_ref.shape[0]):
        total = total + part_ref[j].astype(F32)
    turned = full_turn(total, cos_ref[...], -sin_ref[...])
    left = lax.broadcasted_iota(jnp.int32, total.shape, 1) < 64
    out_ref[...] = jnp.where(left, turned, total).astype(BF16)


def collect(part, cosine, sine):
    shape = jax.ShapeDtypeStruct(part.shape[1:], BF16)
    args = (part, cosine, sine)
    return pl.pallas_call(
        collect_kernel,
        grid=(1,),
        in_specs=[whole(a) for a in args],
        out_specs=whole(shape),
        out_shape=shape,
        compiler_params=pltpu.CompilerParams(vmem_limit_bytes=LIMIT),
        name="collect",
    )(*args)


def finish_kernel(
    me, qm_ref, qo_ref, km_ref, ko_ref, w0, w1, w2, w3, x_ref, gain_ref, da_ref,
    early_ref, gkv_ref, rest_ref, out_ref, small_ref,
):
    xh = me[1]

    def back(q_ref, kv_ref, side, w):
        left = lax.broadcasted_iota(jnp.int32, kv_ref.shape[1:], 1) < 64
        one, two = kv_ref[side].astype(F32), kv_ref[2 + side].astype(F32)
        keys = jnp.where(left, one, pltpu.roll(two, 64, 1)).astype(BF16)
        values = jnp.where(left, pltpu.roll(one, 64, 1), two).astype(BF16)
        return inner(
            jnp.concatenate([q_ref[side], q_ref[2 + side], keys, values], 1), w[...]
        )

    near = back(qm_ref, km_ref, xh, w0) + back(qo_ref, ko_ref, xh, w1)
    far = back(qm_ref, km_ref, 1 - xh, w2) + back(qo_ref, ko_ref, 1 - xh, w3)
    dh1 = near + far
    x = x_ref[...].astype(F32)
    factor = lax.rsqrt(jnp.mean(x * x, -1, keepdims=True) + EPS)
    scaled = dh1 * gain_ref[...]
    out_ref[...] = (
        da_ref[...].astype(F32)
        + factor * scaled
        - x * factor**3 * jnp.mean(scaled * x, -1, keepdims=True)
    ).astype(BF16)
    gain = jnp.sum(dh1 * x * factor, 0, keepdims=True)
    width = gain.shape[1]
    column = jnp.broadcast_to(gain, (128, width)).T
    lane = lax.broadcasted_iota(jnp.int32, (width, 128), 1)
    mark = rest_ref.shape[1] - 1
    small_ref[:, :256] = early_ref[...]
    small_ref[:, 256:384] = gkv_ref[...]
    small_ref[:, 384:] = jnp.where(lane == mark, column, rest_ref[...].astype(F32)).astype(BF16)


def finish(me, qm, qo, km, ko, ws, tokens, gain, da, early, gkv, rest):
    rows, width = tokens.shape
    args = (qm, qo, km, ko, *ws, tokens, gain)
    shapes = [
        jax.ShapeDtypeStruct((rows, width), BF16),
        jax.ShapeDtypeStruct((width, 512), BF16),
    ]
    return pl.pallas_call(
        finish_kernel,
        grid_spec=pltpu.PrefetchScalarGridSpec(
            num_scalar_prefetch=1,
            grid=(1,),
            in_specs=[whole(a) for a in args]
            + [pl.BlockSpec((rows, width), lambda i, me: (me[0], 0))]
            + [whole(a) for a in (early, gkv, rest)],
            out_specs=[whole(a) for a in shapes],
        ),
        out_shape=shapes,
        compiler_params=pltpu.CompilerParams(vmem_limit_bytes=LIMIT),
        name="finish",
    )(me, *args, da, early, gkv, rest)


def on_device(
    tokens,
    cotangent,
    pairing,
    routes,
    norm_attn,
    w_query,
    w_key,
    w_value,
    w_out,
    norm_moe,
    w_router,
    w_gate,
    w_up,
    w_down,
):
    zy = lax.axis_index(ZY)
    xl = lax.axis_index("xl")
    wa = lax.axis_index(WA)
    rows, width = tokens.shape
    block = rows // 2
    both = 2 * rows
    count_ctx = pairing.shape[0]
    blocks = 2 * count_ctx
    groups = count_ctx // 2
    hq = w_query.shape[1] // 2
    hk = w_key.shape[1] // 2
    hall = hq + 2 * hk

    xh = lax.axis_index("xh")
    core = lax.axis_index("c")
    first = wa * w_gate.shape[0] + xl * (w_gate.shape[0] // 2)
    me = jnp.stack([xl, xh, core, first, xl * 4 + wa]).astype(jnp.int32)

    pair = lax.dynamic_slice_in_dim(pairing, zy * 2, 2)
    starts = jnp.stack([pair, blocks - 1 - pair], 1).reshape(4) * block
    qpos = (starts[:, None] + jnp.arange(block, dtype=jnp.int32)[None, :]).reshape(both)

    cos2, sin2 = lane_angles(qpos)
    own = lambda a: lax.dynamic_slice_in_dim(a, xl * rows, rows, 0)
    keep, give = start(
        me, tokens, norm_attn[None], w_query, w_key, w_value, own(cos2), own(sin2)
    )
    got = lax.ppermute(give, "xl", SWAP)
    low = xl == 0
    qkv = jnp.concatenate([jnp.where(low, keep, got), jnp.where(low, got, keep)], 0)
    rq = qkv[:, :hq]
    kv_mine = qkv[:, hq:]

    kv_all = lax.all_to_all(
        jnp.broadcast_to(kv_mine[None], (groups,) + kv_mine.shape), ZY, 0, 0, tiled=False
    ).reshape(blocks, block, 2 * hk)

    def ring_weights(w):
        near = lax.ppermute(w, "c", SWAP)
        far = lax.ppermute(w, "xh", SWAP)
        return w, near, far, lax.ppermute(far, "c", SWAP)

    w_outs = ring_weights(w_out)
    w_ins = ring_weights(jnp.concatenate([w_query, w_key, w_value], 1))

    def ring_parts(w):
        return w, lax.ppermute(w, "c", SWAP), lax.ppermute(w, "xh", SWAP), lax.ppermute(
            w, WA, [(0, 3), (3, 0), (1, 2), (2, 1)]
        )

    def in_order(parts):
        near = jnp.where(core == 0, jnp.concatenate(parts[:2], 0), jnp.concatenate(parts[1::-1], 0))
        far = jnp.where(core == 0, jnp.concatenate(parts[2:], 0), jnp.concatenate(parts[:1:-1], 0))
        return jnp.where(xh == 0, jnp.concatenate([near, far], 0), jnp.concatenate([far, near], 0))

    x_pair = swap_x(tokens)
    dy_pair = swap_x(cotangent)
    routes_pair = swap_x(routes.astype(F32)).astype(jnp.int32)

    ranks = jnp.arange(count_ctx, dtype=jnp.int32)
    inverse = jnp.sum(jnp.where(pairing[None, :] == ranks[:, None], ranks[None, :], 0), 1)
    slot = jnp.concatenate([inverse * 2, inverse[::-1] * 2 + 1])
    place = starts // block
    attn_low, attn, lse, ks, kt = attend(place, slot, rq, kv_all)

    o_mine = lax.all_to_all(
        jnp.broadcast_to(attn_low[None], (4,) + attn_low.shape), CHIPS, 0, 0, tiled=False
    )
    o_other = lax.ppermute(o_mine, "c", SWAP)
    experts_all = w_router.shape[1]
    router = jnp.pad(w_router, ((0, 0), (0, 128 - experts_all)))
    x2, h2, mix_all, keep, give, mkeep, mgive, grads = experts(
        me, o_mine, o_other, x_pair, dy_pair, routes_pair, w_outs, norm_moe[None], router,
        w_gate, w_up, w_down, groups,
    )

    def add(one, two):
        return (one.astype(F32) + two.astype(F32)).astype(BF16)

    part = add(keep, lax.ppermute(give, "c", SWAP))
    part = lax.all_to_all(part, CHIPS, 0, 0, tiled=False)
    grads = lax.psum_scatter(grads, "z", scatter_dimension=0, tiled=True)
    payload = middle(me, part, x2, mix_all, dy_pair, norm_moe[None], router)
    full = lax.all_to_all(payload, CHIPS, 0, 0, tiled=False)
    other = lax.ppermute(full, "c", SWAP)

    moe = add(mkeep, lax.ppermute(mgive, "c", SWAP))
    moe, full = lax.optimization_barrier((moe, full))
    moe = lax.all_to_all(moe, CHIPS, 0, 0, tiled=False)

    dq, grad_kv, da, rest_pair = attend_back(
        place, slot, me, rq, full, other, attn, lse, ks, kt, cos2, sin2, w_out
    )
    few = both // 8
    mine = lambda a: lax.dynamic_slice_in_dim(a, (xl * 4 + wa) * few, few, 0)
    out_rows = (mine(x2) + jnp.sum(moe.astype(F32), 0)).astype(BF16)
    ones = ring_parts(out_rows)
    output = in_order(ones)
    gnm_all = rest_pair[:, experts_all : experts_all + width // few].astype(F32)
    gnm_own = jnp.sum(own(gnm_all).reshape(4, few, width // few), 0).reshape(width)
    grad_kv = lax.all_to_all(
        grad_kv.reshape(groups, both, 2 * hk), ZY, 0, 0, tiled=False
    )
    grad_kv, grads = lax.optimization_barrier((grad_kv, grads))
    grads = lax.psum_scatter(grads, "y", scatter_dimension=0, tiled=True)[0]
    dkv = collect(grad_kv, cos2, sin2)
    h1 = rms(x_pair.astype(F32), norm_attn)[0].astype(BF16)

    def to_rows(piece):
        n = piece.shape[1]
        parts = piece.reshape(2, rows, n)
        same = lax.dynamic_index_in_dim(parts, xl, 0, False)
        swapped = lax.ppermute(lax.dynamic_index_in_dim(parts, 1 - xl, 0, False), "xl", SWAP)
        both_far = lax.ppermute(jnp.stack([same, swapped]), "xh", SWAP)
        here = jnp.where(low, jnp.stack([same, swapped]), jnp.stack([swapped, same]))
        away = jnp.where(low, both_far, both_far[::-1])
        mine = jnp.where(xh == 0, jnp.stack([here, away], 1), jnp.stack([away, here], 1))
        mine = mine.reshape(4, rows, n)
        return mine, lax.ppermute(mine, "c", SWAP)

    def to_rows_now(piece):
        n = piece.shape[1]
        mine = lax.all_to_all(
            jnp.broadcast_to(piece.reshape(2, 1, rows, n), (2, 2, rows, n)).reshape(4, rows, n),
            CHIPS, 0, 0, tiled=False,
        )
        return mine, lax.ppermute(mine, "c", SWAP)

    dq_mine, dq_other = to_rows(dq)
    kv_mine, kv_other = to_rows_now(dkv)
    h2_own = own(h2)
    rest = jnp.concatenate(
        [outer(h2_own, own(rest_pair)[:, :experts_all]), gnm_own[:, None]], 1
    ).astype(BF16)
    rest = jnp.pad(rest, ((0, 0), (0, 128 - rest.shape[1])))
    early = jnp.concatenate([outer(h1, dq), outer(da, attn_low)], 1).astype(BF16)
    gkv = outer(h1, dkv).astype(BF16)
    grad_tokens, small = finish(
        me, dq_mine, dq_other, kv_mine, kv_other, w_ins, tokens, norm_attn[None], da,
        early, gkv, rest,
    )

    local = grads.shape[0]
    nrow = width // groups // 2
    by_dest = jnp.concatenate(
        [
            grads[:, : 2 * nrow].reshape(local, 2, nrow, width),
            grads[:, 2 * nrow :].reshape(local, 2, nrow // 2, width),
        ],
        2,
    ).transpose(1, 0, 2, 3)
    by_dest, small = lax.optimization_barrier((by_dest, small))
    keep_w = lax.dynamic_index_in_dim(by_dest, xl, 0, False)
    got_w = lax.ppermute(lax.dynamic_index_in_dim(by_dest, 1 - xl, 0, False), "xl", SWAP)

    small = lax.all_to_all(small.reshape(count_ctx, -1, small.shape[1]), CTX, 0, 0, tiled=False)
    small = jnp.sum(small.reshape(groups, 2, -1, small.shape[2]).astype(F32), 0)
    def pair_of(a, n):
        return jnp.concatenate([small[0, :, a : a + n], small[1, :, a : a + n]], 1)

    grad_query = pair_of(0, hq)
    grad_out = pair_of(hq, hq).T
    grad_key = pair_of(2 * hq, hk)
    grad_value = pair_of(2 * hq + hk, hk)
    rest = small[0, :, 3 * hq :] + small[1, :, 3 * hq :]
    grad_router = rest[:, :experts_all]
    grad_norm_moe = rest[:, experts_all]
    grad_norm_attn = rest[:, 127]
    pairw = jnp.concatenate(
        [jnp.where(low, keep_w, got_w), jnp.where(low, got_w, keep_w)], 0
    ).astype(F32)
    half = width // 2
    grad_gate = pairw[:, :nrow, :half]
    grad_up = pairw[:, :nrow, half:]
    grad_down = pairw[:, nrow:]
    return (
        output,
        grad_tokens,
        grad_norm_attn,
        grad_query,
        grad_key,
        grad_value,
        grad_out,
        grad_norm_moe,
        grad_router,
        grad_gate,
        grad_up,
        grad_down,
    )


def solution(mesh):
    fine = Mesh(mesh.devices.reshape(4, 4, 2, 2, 2), ("z", "y", "xl", "xh", "c"))
    return jax.shard_map(
        on_device,
        mesh=fine,
        in_specs=(
            P(CTX, None),
            P(CTX, None),
            P(),
            P(CTX, None),
            P(),
            P(None, WA),
            P(None, WA),
            P(None, WA),
            P(WA, None),
            P(),
            P(),
            P(WA, None, None),
            P(WA, None, None),
            P(WA, None, None),
        ),
        out_specs=(
            P(CTX, None),
            P(CTX, None),
            P(CTX),
            P(CTX, WA),
            P(CTX, WA),
            P(CTX, WA),
            P(WA, CTX),
            P(CTX),
            P(CTX, None),
            P(WA, CTX, None),
            P(WA, CTX, None),
            P(WA, CTX, None),
        ),
        check_vma=False,
    )
```

```python
import jax
import jax.numpy as jnp
from jax import lax
from jax.experimental import pallas as pl
from jax.experimental.pallas import tpu as pltpu
from jax.sharding import Mesh
from jax.sharding import PartitionSpec as P

HEAD_DIM = 64
EPS = 1e-05
THETA = 10000.0
CTX = ("z", "y", "xl")
WA = ("xh", "c")
ZY = ("z", "y")
CHIPS = ("xl", "xh")
BF16 = jnp.bfloat16
F32 = jnp.float32
SWAP = [(0, 1), (1, 0)]


def dot(left, right):
    return jnp.dot(left, right, preferred_element_type=F32)


def outer(left, right):
    return lax.dot_general(left, right, (((0,), (0,)), ((), ())), preferred_element_type=F32)


def inner(left, right):
    return lax.dot_general(left, right, (((1,), (1,)), ((), ())), preferred_element_type=F32)


def rms(values, gain):
    factor = lax.rsqrt(jnp.mean(values * values, -1, keepdims=True) + EPS)
    return values * factor * gain, factor


def swap_x(mine):
    other = lax.ppermute(mine, "xl", SWAP)
    low = lax.axis_index("xl") == 0
    return jnp.concatenate([jnp.where(low, mine, other), jnp.where(low, other, mine)], 0)


TILE = 1024
LIMIT = 48 * 1024 * 1024


def full_turn(flat, cosine, sine):
    rows, width = flat.shape
    lane = lax.broadcasted_iota(jnp.int32, (rows, 128), 1)
    first = (lane & 63) < 32
    parts = []
    for n in range(width // 128):
        piece = flat[:, n * 128 : (n + 1) * 128]
        other = jnp.where(first, pltpu.roll(piece, 96, 1), pltpu.roll(piece, 32, 1))
        parts.append(piece * cosine + other * sine)
    return parts[0] if len(parts) == 1 else jnp.concatenate(parts, 1)


def lane_angles(pos):
    lane = jnp.arange(128, dtype=jnp.int32)
    freq = THETA ** (-((lane % 32).astype(F32) * 2.0 / HEAD_DIM))
    angle = pos.astype(F32)[:, None] * freq[None, :]
    sign = jnp.where(lane % 64 < 32, -1.0, 1.0)
    return jnp.cos(angle), jnp.sin(angle) * sign[None, :]


def heads_across(block, low):
    turned = block.T
    both = jnp.concatenate([turned[:64], turned[64:]], 1)
    zero = jnp.zeros_like(both)
    return jnp.concatenate([both, zero] if low == 0 else [zero, both], 0)


def heads_back(both):
    return jnp.concatenate([both[:, :128], both[:, 128:]], 0).T


def turns(place, step, per):
    for pair in (0, 1):
        late = place[2 * pair + 1]
        count = late // per + 1
        first = step < count
        yield (
            jnp.where(first, 2 * pair + 1, 2 * pair),
            jnp.where(first, step, step - count),
            jnp.where(first, late, place[2 * pair]),
        )


def attend_kernel(
    place, slot, q_ref, kv_ref, low_ref, o_ref, lse_ref, ks_ref, kt_ref, query_s, top_s, sum_s, acc_s
):
    per = TILE // 128

    def sort(tile, unused):
        for j in range(per):
            block = kv_ref[slot[tile * per + j]]
            ks_ref[tile, j * 128 : (j + 1) * 128, :] = block
            kt_ref[tile, :, j * 128 : (j + 1) * 128] = block.astype(F32).T.astype(BF16)
        return unused

    lax.fori_loop(0, ks_ref.shape[0], sort, 0)
    apart = lax.broadcasted_iota(jnp.int32, (TILE, 256), 0) - (
        lax.broadcasted_iota(jnp.int32, (TILE, 256), 1) & 127
    )
    count = q_ref.shape[0] // 128
    for b in range(count):
        query = q_ref[b * 128 : (b + 1) * 128, :].astype(F32) * HEAD_DIM**-0.5
        query_s[b] = heads_across(query, 0).astype(BF16)
    top_s[...] = jnp.full(top_s.shape, -1e30, F32)
    sum_s[...] = jnp.zeros(sum_s.shape, F32)
    acc_s[...] = jnp.zeros(acc_s.shape, F32)

    def step(index, unused):
        work = list(turns(place, index, per))
        scores = [
            jnp.where(apart <= own * 128 - tile * TILE, dot(ks_ref[tile], query_s[b]), -1e30)
            for b, tile, own in work
        ]
        for (b, tile, own), score in zip(work, scores):
            top = top_s[b]
            new_top = jnp.maximum(top, jnp.max(score, 0, keepdims=True))
            keep = jnp.exp(top - new_top)
            probs = jnp.exp(score - new_top)
            top_s[b] = new_top
            sum_s[b] = sum_s[b] * keep + jnp.sum(probs, 0, keepdims=True)
            acc_s[b] = acc_s[b] * keep + dot(kt_ref[tile], probs.astype(BF16))
        return unused

    lax.fori_loop(0, ks_ref.shape[0] + 1, step, 0, unroll=3)
    for b in range(count):
        result = acc_s[b][64:] / sum_s[b]
        o_ref[b] = result
        lse_ref[b] = top_s[b] + jnp.log(sum_s[b])
        low_ref[b * 128 : (b + 1) * 128, :] = heads_back(result).astype(BF16)


def attend(place, slot, rq, kv_all):
    count = rq.shape[0] // 128
    tiles = kv_all.shape[0] * 128 // TILE
    return pl.pallas_call(
        attend_kernel,
        grid_spec=pltpu.PrefetchScalarGridSpec(
            num_scalar_prefetch=2,
            grid=(1,),
            in_specs=[
                pl.BlockSpec(rq.shape, lambda i, *_: (0, 0)),
                pl.BlockSpec(kv_all.shape, lambda i, *_: (0, 0, 0)),
            ],
            out_specs=[
                pl.BlockSpec(rq.shape, lambda i, *_: (0, 0)),
                pl.BlockSpec((count, 64, 256), lambda i, *_: (0, 0, 0)),
                pl.BlockSpec((count, 1, 256), lambda i, *_: (0, 0, 0)),
                pl.BlockSpec((tiles, TILE, 128), lambda i, *_: (0, 0, 0)),
                pl.BlockSpec((tiles, 128, TILE), lambda i, *_: (0, 0, 0)),
            ],
            scratch_shapes=[
                pltpu.VMEM((count, 128, 256), BF16),
                pltpu.VMEM((count, 1, 256), F32),
                pltpu.VMEM((count, 1, 256), F32),
                pltpu.VMEM((count, 128, 256), F32),
            ],
        ),
        out_shape=[
            jax.ShapeDtypeStruct(rq.shape, BF16),
            jax.ShapeDtypeStruct((count, 64, 256), F32),
            jax.ShapeDtypeStruct((count, 1, 256), F32),
            jax.ShapeDtypeStruct((tiles, TILE, 128), BF16),
            jax.ShapeDtypeStruct((tiles, 128, TILE), BF16),
        ],
        compiler_params=pltpu.CompilerParams(vmem_limit_bytes=LIMIT),
        cost_estimate=pl.CostEstimate(
            flops=20_000_000_000, bytes_accessed=8_000_000, transcendentals=4_000_000
        ),
        name="attend",
    )(place, slot, rq, kv_all)


def attend_back_kernel(
    place, slot, me, q_ref, full_ref, other_ref, o_ref, lse_ref, ks_ref, kt_ref, cos_ref, sin_ref, wo_ref,
    dq_ref, dkv_ref, da_ref, rest_ref, acc_ref, right_s, under_s, delta_s, dq_s,
):
    per = TILE // 128

    def clear(tile, unused):
        acc_ref[tile] = jnp.zeros((TILE, 128), F32)
        return unused

    lax.fori_loop(0, acc_ref.shape[0], clear, 0)
    few, width = full_ref.shape[1], da_ref.shape[1]
    for b in range(full_ref.shape[0]):
        for ref, side in ((full_ref, me[2]), (other_ref, 1 - me[2])):
            at = pl.ds(pl.multiple_of(b * 2 * few + side * few, few), few)
            da_ref[at, :] = ref[b, :, :width]
            rest_ref[at, :] = ref[b, :, width:]
    apart = lax.broadcasted_iota(jnp.int32, (TILE, 256), 0) - (
        lax.broadcasted_iota(jnp.int32, (TILE, 256), 1) & 127
    )
    count = q_ref.shape[0] // 128
    for b in range(count):
        sl = slice(b * 128, (b + 1) * 128)
        query = heads_across(q_ref[sl, :].astype(F32) * HEAD_DIM**-0.5, 0)
        grad = inner(da_ref[sl, :], wo_ref[...]).astype(BF16)
        grad = heads_across(grad.astype(F32), 64)
        delta_s[b] = jnp.sum(grad[64:] * o_ref[b], 0, keepdims=True)
        right_s[b] = jnp.concatenate([query, grad], 1).astype(BF16)
        under_s[b] = jnp.concatenate([query.T, grad.T], 0).astype(BF16)
    dq_s[...] = jnp.zeros(dq_s.shape, F32)

    def step(index, unused):
        work = list(turns(place, index, per))
        prods = [dot(ks_ref[tile], right_s[b]) for b, tile, own in work]
        sides = []
        for (b, tile, own), prod in zip(work, prods):
            probs = jnp.exp(prod[:, :256] - lse_ref[b])
            probs = jnp.where(apart <= own * 128 - tile * TILE, probs, 0.0)
            dscore = (probs * (prod[:, 256:] - delta_s[b])).astype(BF16)
            sides.append(jnp.concatenate([dscore, probs.astype(BF16)], 1))
        for (b, tile, own), side in zip(work, sides):
            acc_ref[tile] += dot(side, under_s[b])
            dq_s[b] += dot(kt_ref[tile], side[:, :256])
        return unused

    lax.fori_loop(0, ks_ref.shape[0] + 1, step, 0, unroll=3)
    for b in range(count):
        sl = slice(b * 128, (b + 1) * 128)
        dq = heads_back(dq_s[b][:64]) * HEAD_DIM**-0.5
        dq_ref[sl, :] = full_turn(dq, cos_ref[sl, :], -sin_ref[sl, :]).astype(BF16)

    def unsort(tile, unused):
        for j in range(per):
            dkv_ref[slot[tile * per + j]] = acc_ref[tile, j * 128 : (j + 1) * 128, :].astype(BF16)
        return unused

    lax.fori_loop(0, acc_ref.shape[0], unsort, 0)


def attend_back(place, slot, me, rq, full, other, o, lse, ks, kt, cosine, sine, w_out):
    rows = rq.shape[0]
    width = w_out.shape[1]
    blocks = slot.shape[0]
    args = (rq, full, other, o, lse, ks, kt, cosine, sine)
    shapes = [
        jax.ShapeDtypeStruct(rq.shape, BF16),
        jax.ShapeDtypeStruct((blocks, 128, 128), BF16),
        jax.ShapeDtypeStruct((rows, width), BF16),
        jax.ShapeDtypeStruct((rows, 128), BF16),
    ]
    return pl.pallas_call(
        attend_back_kernel,
        grid_spec=pltpu.PrefetchScalarGridSpec(
            num_scalar_prefetch=3,
            grid=(1,),
            in_specs=[whole(a) for a in args]
            + [pl.BlockSpec((rq.shape[1], width), lambda i, place, slot, me: (me[0], 0))],
            out_specs=[whole(a) for a in shapes],
            scratch_shapes=[
                pltpu.VMEM(ks.shape, F32),
                pltpu.VMEM((rows // 128, 128, 512), BF16),
                pltpu.VMEM((rows // 128, 512, 128), BF16),
                pltpu.VMEM((rows // 128, 1, 256), F32),
                pltpu.VMEM((rows // 128, 128, 256), F32),
            ],
        ),
        out_shape=shapes,
        compiler_params=pltpu.CompilerParams(vmem_limit_bytes=LIMIT),
        cost_estimate=pl.CostEstimate(
            flops=30_000_000_000, bytes_accessed=8_000_000, transcendentals=4_000_000
        ),
        name="attend_back",
    )(place, slot, me, *args, w_out)


def whole(a):
    rank = len(a.shape)
    return pl.BlockSpec(a.shape, lambda i, *_: (0,) * rank, pipeline_mode=pl.Buffered(1))


def experts_kernel(
    me, o_ref, p_ref, x_ref, dy_ref, routes_ref, wo0, wo1, wo2, wo3, gain_ref, wr_ref,
    wg_ref, wu_ref, wd_ref,
    x2_ref, h2_ref, mix_ref, keep_ref, give_ref, mkeep_ref, mgive_ref, grad_ref,
    dh2_acc, moe_acc, dmix_acc,
):
    step = pl.program_id(0)
    xh, core, first = me[1], me[2], me[3]
    rows = x_ref.shape[0]
    lane = lax.broadcasted_iota(jnp.int32, (rows, 128), 1)

    @pl.when(step == 0)
    def _():
        def heads(ref, side):
            return jnp.concatenate([ref[side], ref[2 + side]], 1)

        near = dot(heads(o_ref, xh), wo0[...]) + dot(heads(p_ref, xh), wo1[...])
        far = dot(heads(o_ref, 1 - xh), wo2[...]) + dot(heads(p_ref, 1 - xh), wo3[...])
        x2 = x_ref[...].astype(F32) + (near + far)
        x2_ref[...] = x2
        h2 = rms(x2, gain_ref[...])[0].astype(BF16)
        h2_ref[...] = h2
        logits = dot(h2, wr_ref[...])
        routes = routes_ref[...]
        used = lane == routes[:, 0:1]
        for k in range(1, routes.shape[1]):
            used = jnp.logical_or(used, lane == routes[:, k : k + 1])
        top = jnp.max(jnp.where(used, logits, -jnp.inf), 1, keepdims=True)
        expd = jnp.where(used, jnp.exp(logits - top), 0.0)
        mix_ref[...] = expd / jnp.sum(expd, 1, keepdims=True)
        dh2_acc[...] = jnp.zeros_like(dh2_acc)
        moe_acc[...] = jnp.zeros_like(moe_acc)
        dmix_acc[...] = jnp.zeros_like(dmix_acc)

    here = lane == first + step
    gate = jnp.sum(jnp.where(here, mix_ref[...], 0.0), 1, keepdims=True)
    h2 = h2_ref[...]
    dy = dy_ref[...].astype(F32)
    ga = dot(h2, wg_ref[0])
    up = dot(h2, wu_ref[0])
    sig = jax.nn.sigmoid(ga)
    act = ga * sig
    hid = (act * up).astype(BF16)
    eo = dot(hid, wd_ref[0])
    moe_acc[...] += gate * eo
    dmix_acc[...] += jnp.where(here, jnp.sum(dy * eo, 1, keepdims=True), 0.0)
    deo = (gate * dy).astype(BF16)
    dhid = inner(deo, wd_ref[0])
    dga = (dhid * up * (sig * (1.0 + ga * (1.0 - sig)))).astype(BF16)
    dup = (dhid * act).astype(BF16)
    dh2_acc[...] += inner(dga, wg_ref[0]) + inner(dup, wu_ref[0])
    groups = grad_ref.shape[0]
    across = grad_ref.shape[2] * 2 // 3
    width = h2.shape[1]
    grad_ref[:, 0, :across, :512] = outer(h2, dga).astype(BF16).reshape(groups, across, 512)
    grad_ref[:, 0, :across, 512:] = outer(h2, dup).astype(BF16).reshape(groups, across, 512)
    grad_ref[:, 0, across:, :] = outer(hid, deo).astype(BF16).reshape(groups, across // 2, width)

    @pl.when(step == pl.num_programs(0) - 1)
    def _():
        few = rows // 8
        for j in range(4):
            for side, out, mout in ((core, keep_ref, mkeep_ref), (1 - core, give_ref, mgive_ref)):
                at = pl.ds(pl.multiple_of((j * 2 + side) * few, few), few)
                out[j, :, :width] = dh2_acc[at, :].astype(BF16)
                out[j, :, width:] = dmix_acc[at, :].astype(BF16)
                mout[j] = moe_acc[at, :].astype(BF16)


def experts(me, o_mine, o_other, x_pair, dy_pair, routes, wo, gain, router, wg, wu, wd, groups):
    rows, width = x_pair.shape
    few = rows // 8
    local = wg.shape[0] // 2
    ff = wg.shape[2]
    args = (o_mine, o_other, x_pair, dy_pair, routes, *wo, gain, router)
    across = width // groups
    shapes = [
        jax.ShapeDtypeStruct((rows, width), F32),
        jax.ShapeDtypeStruct((rows, width), BF16),
        jax.ShapeDtypeStruct((rows, 128), F32),
        jax.ShapeDtypeStruct((4, few, width + 128), BF16),
        jax.ShapeDtypeStruct((4, few, width + 128), BF16),
        jax.ShapeDtypeStruct((4, few, width), BF16),
        jax.ShapeDtypeStruct((4, few, width), BF16),
    ]
    pick = lambda i, me: (me[0] * local + i, 0, 0)
    return pl.pallas_call(
        experts_kernel,
        grid_spec=pltpu.PrefetchScalarGridSpec(
            num_scalar_prefetch=1,
            grid=(local,),
            in_specs=[whole(a) for a in args]
            + [
                pl.BlockSpec((1, width, ff), pick),
                pl.BlockSpec((1, width, ff), pick),
                pl.BlockSpec((1, ff, width), pick),
            ],
            out_specs=[whole(a) for a in shapes]
            + [pl.BlockSpec((groups, 1, across * 3 // 2, width), lambda i, me: (0, i, 0, 0))],
            scratch_shapes=[
                pltpu.VMEM((rows, width), F32),
                pltpu.VMEM((rows, width), F32),
                pltpu.VMEM((rows, 128), F32),
            ],
        ),
        out_shape=shapes
        + [jax.ShapeDtypeStruct((groups, local, across * 3 // 2, width), BF16)],
        compiler_params=pltpu.CompilerParams(vmem_limit_bytes=56 * 1024 * 1024),
        cost_estimate=pl.CostEstimate(
            flops=20_000_000_000, bytes_accessed=20_000_000, transcendentals=1_000_000
        ),
        name="experts",
    )(me, *args, wg, wu, wd)


def start_kernel(me, x_ref, gain_ref, wq_ref, wk_ref, wv_ref, cos_ref, sin_ref, keep_ref, give_ref):
    h1 = rms(x_ref[...].astype(F32), gain_ref[...])[0].astype(BF16)
    cosine, sine = cos_ref[...], sin_ref[...]
    query = full_turn(dot(h1, wq_ref[...]), cosine, sine)
    key = full_turn(dot(h1, wk_ref[...]), cosine, sine)
    value = dot(h1, wv_ref[...])
    left = lax.broadcasted_iota(jnp.int32, key.shape, 1) < 64
    halves = [
        jnp.concatenate([query[:, :128], jnp.where(left, key, pltpu.roll(value, 64, 1))], 1),
        jnp.concatenate([query[:, 128:], jnp.where(left, pltpu.roll(key, 64, 1), value)], 1),
    ]
    low = me[0] == 0
    keep_ref[...] = jnp.where(low, halves[0], halves[1]).astype(BF16)
    give_ref[...] = jnp.where(low, halves[1], halves[0]).astype(BF16)


def start(me, tokens, gain, wq, wk, wv, cosine, sine):
    args = (tokens, gain, wq, wk, wv, cosine, sine)
    shapes = [jax.ShapeDtypeStruct((tokens.shape[0], 256), BF16)] * 2
    return pl.pallas_call(
        start_kernel,
        grid_spec=pltpu.PrefetchScalarGridSpec(
            num_scalar_prefetch=1,
            grid=(1,),
            in_specs=[whole(a) for a in args],
            out_specs=[whole(a) for a in shapes],
        ),
        out_shape=shapes,
        compiler_params=pltpu.CompilerParams(vmem_limit_bytes=60 * 1024 * 1024),
        name="start",
    )(me, *args)


def middle_kernel(me, part_ref, x2_ref, mix_ref, dy_ref, gain_ref, wr_ref, out_ref):
    part = part_ref[0].astype(F32)
    for j in range(1, part_ref.shape[0]):
        part = part + part_ref[j].astype(F32)
    width = x2_ref.shape[1]
    mix, dmix = mix_ref[...], part[:, width:]
    dlogits = (mix * (dmix - jnp.sum(mix * dmix, 1, keepdims=True))).astype(BF16)
    dh2 = part[:, :width] + inner(dlogits, wr_ref[...])
    x2 = x2_ref[...]
    factor = lax.rsqrt(jnp.mean(x2 * x2, -1, keepdims=True) + EPS)
    scaled = dh2 * gain_ref[...]
    dx2 = dy_ref[...].astype(F32) + (
        factor * scaled - x2 * factor**3 * jnp.mean(scaled * x2, -1, keepdims=True)
    )
    gain = jnp.sum(dh2 * x2 * factor, 0, keepdims=True).astype(BF16).astype(F32)
    rows = x2.shape[0]
    per = width // rows
    at = lax.broadcasted_iota(jnp.int32, (rows, width), 1)
    spread = jnp.where(at // per == lax.broadcasted_iota(jnp.int32, (rows, width), 0), gain, 0.0)
    lane = lax.broadcasted_iota(jnp.int32, (width, 128), 1)
    place = lane == lax.broadcasted_iota(jnp.int32, (width, 128), 0) % per + 16
    extra = dot(spread.astype(BF16), place.astype(F32).astype(BF16)) + dlogits.astype(F32)
    for j in range(out_ref.shape[0]):
        out_ref[j, :, :width] = dx2.astype(BF16)
        out_ref[j, :, width:] = extra.astype(BF16)


def middle(me, part, x2, mix, dy, gain, router):
    few = part.shape[1]
    width = x2.shape[1]
    mine = lambda i, me: (me[4], 0)
    shape = jax.ShapeDtypeStruct(part.shape, BF16)
    return pl.pallas_call(
        middle_kernel,
        grid_spec=pltpu.PrefetchScalarGridSpec(
            num_scalar_prefetch=1,
            grid=(1,),
            in_specs=[
                whole(part),
                pl.BlockSpec((few, width), mine),
                pl.BlockSpec((few, 128), mine),
                pl.BlockSpec((few, width), mine),
                whole(gain),
                whole(router),
            ],
            out_specs=whole(shape),
        ),
        out_shape=shape,
        compiler_params=pltpu.CompilerParams(vmem_limit_bytes=60 * 1024 * 1024),
        name="middle",
    )(me, part, x2, mix, dy, gain, router)


def collect_kernel(part_ref, cos_ref, sin_ref, out_ref):
    total = part_ref[0].astype(F32)
    for j in range(1, part_ref.shape[0]):
        total = total + part_ref[j].astype(F32)
    turned = full_turn(total, cos_ref[...], -sin_ref[...])
    left = lax.broadcasted_iota(jnp.int32, total.shape, 1) < 64
    out_ref[...] = jnp.where(left, turned, total).astype(BF16)


def collect(part, cosine, sine):
    shape = jax.ShapeDtypeStruct(part.shape[1:], BF16)
    args = (part, cosine, sine)
    return pl.pallas_call(
        collect_kernel,
        grid=(1,),
        in_specs=[whole(a) for a in args],
        out_specs=whole(shape),
        out_shape=shape,
        compiler_params=pltpu.CompilerParams(vmem_limit_bytes=LIMIT),
        name="collect",
    )(*args)


def finish_kernel(
    me, m_ref, o_ref, w0, w1, w2, w3, x_ref, gain_ref, da_ref,
    early_ref, gkv_ref, rest_ref, out_ref, small_ref,
):
    xh = me[1]

    def back(ref, side, w):
        one, two = ref[side], ref[2 + side]
        hq = one.shape[1] // 2
        left = lax.broadcasted_iota(jnp.int32, (one.shape[0], hq), 1) < 64
        low, high = one[:, hq:].astype(F32), two[:, hq:].astype(F32)
        keys = jnp.where(left, low, pltpu.roll(high, 64, 1)).astype(BF16)
        values = jnp.where(left, pltpu.roll(low, 64, 1), high).astype(BF16)
        return inner(jnp.concatenate([one[:, :hq], two[:, :hq], keys, values], 1), w[...])

    near = back(m_ref, xh, w0) + back(o_ref, xh, w1)
    far = back(m_ref, 1 - xh, w2) + back(o_ref, 1 - xh, w3)
    dh1 = near + far
    x = x_ref[...].astype(F32)
    factor = lax.rsqrt(jnp.mean(x * x, -1, keepdims=True) + EPS)
    scaled = dh1 * gain_ref[...]
    out_ref[...] = (
        da_ref[...].astype(F32)
        + factor * scaled
        - x * factor**3 * jnp.mean(scaled * x, -1, keepdims=True)
    ).astype(BF16)
    gain = jnp.sum(dh1 * x * factor, 0, keepdims=True)
    width = gain.shape[1]
    column = jnp.broadcast_to(gain, (128, width)).T
    lane = lax.broadcasted_iota(jnp.int32, (width, 128), 1)
    mark = rest_ref.shape[1] - 1
    small_ref[:, :256] = early_ref[...]
    small_ref[:, 256:384] = gkv_ref[...]
    small_ref[:, 384:] = jnp.where(lane == mark, column, rest_ref[...].astype(F32)).astype(BF16)


def finish(me, mine, other, ws, tokens, gain, da, early, gkv, rest):
    rows, width = tokens.shape
    args = (mine, other, *ws, tokens, gain)
    shapes = [
        jax.ShapeDtypeStruct((rows, width), BF16),
        jax.ShapeDtypeStruct((width, 512), BF16),
    ]
    return pl.pallas_call(
        finish_kernel,
        grid_spec=pltpu.PrefetchScalarGridSpec(
            num_scalar_prefetch=1,
            grid=(1,),
            in_specs=[whole(a) for a in args]
            + [pl.BlockSpec((rows, width), lambda i, me: (me[0], 0))]
            + [whole(a) for a in (early, gkv, rest)],
            out_specs=[whole(a) for a in shapes],
        ),
        out_shape=shapes,
        compiler_params=pltpu.CompilerParams(vmem_limit_bytes=LIMIT),
        name="finish",
    )(me, *args, da, early, gkv, rest)


def unpack_kernel(
    me, part_ref, keep_ref, got_ref, own_ref, near_ref, far_ref, last_ref,
    q_ref, k_ref, v_ref, o_ref, r_ref, nm_ref, na_ref, gate_ref, up_ref, down_ref, out_ref,
):
    local, few = keep_ref.shape[0], own_ref.shape[0]
    for ref, side in ((keep_ref, me[0]), (got_ref, 1 - me[0])):
        for e in range(local):
            gate_ref[side * local + e] = ref[e, : gate_ref.shape[1], : gate_ref.shape[2]].astype(F32)
            up_ref[side * local + e] = ref[e, : gate_ref.shape[1], gate_ref.shape[2] :].astype(F32)
            down_ref[side * local + e] = ref[e, gate_ref.shape[1] :, :].astype(F32)
    for ref, xh, core in (
        (own_ref, me[1], me[2]),
        (near_ref, me[1], 1 - me[2]),
        (far_ref, 1 - me[1], me[2]),
        (last_ref, 1 - me[1], 1 - me[2]),
    ):
        out_ref[pl.ds(pl.multiple_of((xh * 2 + core) * few, few), few), :] = ref[...]
    groups = part_ref.shape[0] // 2
    sums = []
    for side in (0, 1):
        total = part_ref[side].astype(F32)
        for j in range(1, groups):
            total = total + part_ref[2 * j + side].astype(F32)
        sums.append(total)
    one, two = sums
    q_ref[...] = jnp.concatenate([one[:, :128], two[:, :128]], 1)
    o_ref[...] = jnp.concatenate([one[:, 128:256], two[:, 128:256]], 1)
    left = lax.broadcasted_iota(jnp.int32, (one.shape[0], 128), 1) < 64
    low, high = one[:, 256:384], two[:, 256:384]
    k_ref[...] = jnp.where(left, low, pltpu.roll(high, 64, 1))
    v_ref[...] = jnp.where(left, pltpu.roll(low, 64, 1), high)
    rest = one[:, 384:] + two[:, 384:]
    rest = jnp.concatenate([rest, jnp.zeros((128 - rest.shape[0], 128), F32)], 0).T
    rows = q_ref.shape[0]
    count = r_ref.shape[0]
    r_ref[...] = rest[:count, :rows]
    nm_ref[...] = rest[count : count + 1, :rows]
    na_ref[...] = rest[127:, :rows]


def unpack(me, part, keep, got, outs, experts_all):
    rows = part.shape[1]
    local, width = keep.shape[0], keep.shape[2]
    args = (part, keep, got, *outs)
    shapes = [
        jax.ShapeDtypeStruct(n, F32)
        for n in (
            (rows, 256), (rows, 128), (rows, 128), (rows, 256), (experts_all, rows), (1, rows), (1, rows),
            (2 * local, rows, width // 2), (2 * local, rows, width // 2), (2 * local, rows // 2, width),
        )
    ] + [jax.ShapeDtypeStruct((4 * outs[0].shape[0], width), BF16)]
    return pl.pallas_call(
        unpack_kernel,
        grid_spec=pltpu.PrefetchScalarGridSpec(
            num_scalar_prefetch=1,
            grid=(1,),
            in_specs=[whole(a) for a in args],
            out_specs=[whole(a) for a in shapes],
        ),
        out_shape=shapes,
        compiler_params=pltpu.CompilerParams(vmem_limit_bytes=LIMIT),
        name="unpack",
    )(me, *args)


def on_device(
    tokens,
    cotangent,
    pairing,
    routes,
    norm_attn,
    w_query,
    w_key,
    w_value,
    w_out,
    norm_moe,
    w_router,
    w_gate,
    w_up,
    w_down,
):
    zy = lax.axis_index(ZY)
    xl = lax.axis_index("xl")
    wa = lax.axis_index(WA)
    rows, width = tokens.shape
    block = rows // 2
    both = 2 * rows
    count_ctx = pairing.shape[0]
    blocks = 2 * count_ctx
    groups = count_ctx // 2
    hq = w_query.shape[1] // 2
    hk = w_key.shape[1] // 2
    hall = hq + 2 * hk

    xh = lax.axis_index("xh")
    core = lax.axis_index("c")
    first = wa * w_gate.shape[0] + xl * (w_gate.shape[0] // 2)
    me = jnp.stack([xl, xh, core, first, xl * 4 + wa]).astype(jnp.int32)

    pair = lax.dynamic_slice_in_dim(pairing, zy * 2, 2)
    starts = jnp.stack([pair, blocks - 1 - pair], 1).reshape(4) * block
    qpos = (starts[:, None] + jnp.arange(block, dtype=jnp.int32)[None, :]).reshape(both)

    cos2, sin2 = lane_angles(qpos)
    own = lambda a: lax.dynamic_slice_in_dim(a, xl * rows, rows, 0)
    keep, give = start(
        me, tokens, norm_attn[None], w_query, w_key, w_value, own(cos2), own(sin2)
    )
    got = lax.ppermute(give, "xl", SWAP)
    low = xl == 0
    qkv = jnp.concatenate([jnp.where(low, keep, got), jnp.where(low, got, keep)], 0)
    rq = qkv[:, :hq]
    kv_mine = qkv[:, hq:]

    kv_all = lax.all_to_all(
        jnp.broadcast_to(kv_mine[None], (groups,) + kv_mine.shape), ZY, 0, 0, tiled=False
    ).reshape(blocks, block, 2 * hk)

    def ring_weights(w):
        near = lax.ppermute(w, "c", SWAP)
        far = lax.ppermute(w, "xh", SWAP)
        return w, near, far, lax.ppermute(far, "c", SWAP)

    w_outs = ring_weights(w_out)
    w_in = jnp.concatenate([w_query, w_key, w_value], 1)

    def ring_parts(w):
        return w, lax.ppermute(w, "c", SWAP), lax.ppermute(w, "xh", SWAP), lax.ppermute(
            w, WA, [(0, 3), (3, 0), (1, 2), (2, 1)]
        )

    x_pair = swap_x(tokens)
    routes_pair = swap_x(routes.astype(F32)).astype(jnp.int32)
    h1 = rms(x_pair.astype(F32), norm_attn)[0].astype(BF16)
    kv_all, x_pair, routes_pair, h1, cotangent = lax.optimization_barrier(
        (kv_all, x_pair, routes_pair, h1, cotangent)
    )
    dy_pair = swap_x(cotangent)

    ranks = jnp.arange(count_ctx, dtype=jnp.int32)
    inverse = jnp.sum(jnp.where(pairing[None, :] == ranks[:, None], ranks[None, :], 0), 1)
    slot = jnp.concatenate([inverse * 2, inverse[::-1] * 2 + 1])
    place = starts // block
    attn_low, attn, lse, ks, kt = attend(place, slot, rq, kv_all)
    attn_low, dy_pair, w_outs = lax.optimization_barrier((attn_low, dy_pair, w_outs))

    o_mine = lax.all_to_all(
        jnp.broadcast_to(attn_low[None], (4,) + attn_low.shape), CHIPS, 0, 0, tiled=False
    )
    o_other = lax.ppermute(o_mine, "c", SWAP)
    experts_all = w_router.shape[1]
    router = jnp.pad(w_router, ((0, 0), (0, 128 - experts_all)))
    x2, h2, mix_all, keep, give, mkeep, mgive, grads = experts(
        me, o_mine, o_other, x_pair, dy_pair, routes_pair, w_outs, norm_moe[None], router,
        w_gate, w_up, w_down, groups,
    )

    def add(one, two):
        return (one.astype(F32) + two.astype(F32)).astype(BF16)

    part = add(keep, lax.ppermute(give, "c", SWAP))
    part = lax.all_to_all(part, CHIPS, 0, 0, tiled=False)
    grads = lax.psum_scatter(grads, "z", scatter_dimension=0, tiled=True)
    payload = middle(me, part, x2, mix_all, dy_pair, norm_moe[None], router)
    full = lax.all_to_all(payload, CHIPS, 0, 0, tiled=False)
    other = lax.ppermute(full, "c", SWAP)

    full, w_in = lax.optimization_barrier((full, w_in))
    w_ins = ring_weights(w_in)

    dq, grad_kv, da, rest_pair = attend_back(
        place, slot, me, rq, full, other, attn, lse, ks, kt, cos2, sin2, w_out
    )
    grad_kv, mkeep, mgot = lax.optimization_barrier(
        (grad_kv, mkeep, lax.ppermute(mgive, "c", SWAP))
    )
    moe = add(mkeep, mgot).reshape(2, 2, both // 8, width)
    at = lambda a, b: lax.dynamic_index_in_dim(
        lax.dynamic_index_in_dim(moe, a, 0, False), b, 0, False
    )
    few = both // 8
    moe_rows = (
        at(xl, xh).astype(F32)
        + lax.ppermute(at(1 - xl, xh), "xl", SWAP).astype(F32)
        + lax.ppermute(at(xl, 1 - xh), "xh", SWAP).astype(F32)
        + lax.ppermute(at(1 - xl, 1 - xh), CHIPS, [(0, 3), (3, 0), (1, 2), (2, 1)]).astype(F32)
    )
    out_rows = (lax.dynamic_slice_in_dim(x2, me[4] * few, few, 0) + moe_rows).astype(BF16)
    gnm_all = rest_pair[:, experts_all : experts_all + width // few].astype(F32)
    gnm_own = jnp.sum(own(gnm_all).reshape(4, few, width // few), 0).reshape(width)
    grad_kv = lax.all_to_all(
        grad_kv.reshape(groups, both, 2 * hk), ZY, 0, 0, tiled=False
    )
    h2_own = own(h2)
    rest = jnp.concatenate(
        [outer(h2_own, own(rest_pair)[:, :experts_all]), gnm_own[:, None]], 1
    ).astype(BF16)
    rest = jnp.pad(rest, ((0, 0), (0, 128 - rest.shape[1])))
    early = jnp.concatenate([outer(h1, dq), outer(da, attn_low)], 1).astype(BF16)
    grad_kv, rest, early, out_rows, w_ins, grads = lax.optimization_barrier(
        (grad_kv, rest, early, out_rows, w_ins, grads)
    )
    grads = lax.psum_scatter(grads, "y", scatter_dimension=0, tiled=True)[0]
    dkv = collect(grad_kv, cos2, sin2)

    def to_rows(piece):
        n = piece.shape[1]
        mine = lax.all_to_all(
            jnp.broadcast_to(piece.reshape(2, 1, rows, n), (2, 2, rows, n)).reshape(4, rows, n),
            CHIPS, 0, 0, tiled=False,
        )
        return mine, lax.ppermute(mine, "c", SWAP)

    d_mine, d_other = to_rows(jnp.concatenate([dq, dkv], 1))
    gkv = outer(h1, dkv).astype(BF16)
    grad_tokens, small = finish(
        me, d_mine, d_other, w_ins, tokens, norm_attn[None], da,
        early, gkv, rest,
    )

    local = grads.shape[0]
    nrow = width // groups // 2
    by_dest = jnp.concatenate(
        [
            grads[:, : 2 * nrow].reshape(local, 2, nrow, width),
            grads[:, 2 * nrow :].reshape(local, 2, nrow // 2, width),
        ],
        2,
    ).transpose(1, 0, 2, 3)
    by_dest, small, out_rows = lax.optimization_barrier((by_dest, small, out_rows))
    outs = ring_parts(out_rows)
    keep_w = lax.dynamic_index_in_dim(by_dest, xl, 0, False)
    got_w = lax.ppermute(lax.dynamic_index_in_dim(by_dest, 1 - xl, 0, False), "xl", SWAP)

    small = lax.all_to_all(small.reshape(count_ctx, -1, small.shape[1]), CTX, 0, 0, tiled=False)
    (
        grad_query, grad_key, grad_value, grad_out, grad_router, gnm, gna, grad_gate, grad_up,
        grad_down, output,
    ) = unpack(me, small, keep_w, got_w, outs, experts_all)
    grad_out, grad_router = grad_out.T, grad_router.T
    grad_norm_moe, grad_norm_attn = gnm.reshape(-1), gna.reshape(-1)
    return (
        output,
        grad_tokens,
        grad_norm_attn,
        grad_query,
        grad_key,
        grad_value,
        grad_out,
        grad_norm_moe,
        grad_router,
        grad_gate,
        grad_up,
        grad_down,
    )


def solution(mesh):
    fine = Mesh(mesh.devices.reshape(4, 4, 2, 2, 2), ("z", "y", "xl", "xh", "c"))
    return jax.shard_map(
        on_device,
        mesh=fine,
        in_specs=(
            P(CTX, None),
            P(CTX, None),
            P(),
            P(CTX, None),
            P(),
            P(None, WA),
            P(None, WA),
            P(None, WA),
            P(WA, None),
            P(),
            P(),
            P(WA, None, None),
            P(WA, None, None),
            P(WA, None, None),
        ),
        out_specs=(
            P(CTX, None),
            P(CTX, None),
            P(CTX),
            P(CTX, WA),
            P(CTX, WA),
            P(CTX, WA),
            P(WA, CTX),
            P(CTX),
            P(CTX, None),
            P(WA, CTX, None),
            P(WA, CTX, None),
            P(WA, CTX, None),
        ),
        check_vma=False,
    )
```

```python
import jax
import jax.numpy as jnp
from jax import lax
from jax.experimental import pallas as pl
from jax.experimental.pallas import tpu as pltpu
from jax.sharding import Mesh
from jax.sharding import PartitionSpec as P

HEAD_DIM = 64
EPS = 1e-05
THETA = 10000.0
CTX = ("z", "y", "xl")
WA = ("xh", "c")
ZY = ("z", "y")
CHIPS = ("xl", "xh")
BF16 = jnp.bfloat16
F32 = jnp.float32
SWAP = [(0, 1), (1, 0)]


def dot(left, right):
    return jnp.dot(left, right, preferred_element_type=F32)


def outer(left, right):
    return lax.dot_general(left, right, (((0,), (0,)), ((), ())), preferred_element_type=F32)


def inner(left, right):
    return lax.dot_general(left, right, (((1,), (1,)), ((), ())), preferred_element_type=F32)


def rms(values, gain):
    factor = lax.rsqrt(jnp.mean(values * values, -1, keepdims=True) + EPS)
    return values * factor * gain, factor


def swap_x(mine):
    return in_pair(mine, lax.ppermute(mine, "xl", SWAP))


def in_pair(mine, other):
    low = lax.axis_index("xl") == 0
    return jnp.concatenate([jnp.where(low, mine, other), jnp.where(low, other, mine)], 0)


TILE = 1024
LIMIT = 40 * 1024 * 1024
EXPERT_LIMIT = 56 * 1024 * 1024


def full_turn(flat, cosine, sine):
    rows, width = flat.shape
    lane = lax.broadcasted_iota(jnp.int32, (rows, 128), 1)
    first = (lane & 63) < 32
    parts = []
    for n in range(width // 128):
        piece = flat[:, n * 128 : (n + 1) * 128]
        other = jnp.where(first, pltpu.roll(piece, 96, 1), pltpu.roll(piece, 32, 1))
        parts.append(piece * cosine + other * sine)
    return parts[0] if len(parts) == 1 else jnp.concatenate(parts, 1)


def lane_angles(pos):
    lane = jnp.arange(128, dtype=jnp.int32)
    freq = THETA ** (-((lane % 32).astype(F32) * 2.0 / HEAD_DIM))
    angle = pos.astype(F32)[:, None] * freq[None, :]
    sign = jnp.where(lane % 64 < 32, -1.0, 1.0)
    return jnp.cos(angle), jnp.sin(angle) * sign[None, :]


def heads_across(block, low):
    turned = block.T
    both = jnp.concatenate([turned[:64], turned[64:]], 1)
    zero = jnp.zeros_like(both)
    return jnp.concatenate([both, zero] if low == 0 else [zero, both], 0)


def heads_back(both):
    return jnp.concatenate([both[:, :128], both[:, 128:]], 0).T


def turns(place, step, per):
    for pair in (0, 1):
        late = place[2 * pair + 1]
        count = late // per + 1
        first = step < count
        yield (
            jnp.where(first, 2 * pair + 1, 2 * pair),
            jnp.where(first, step, step - count),
            jnp.where(first, late, place[2 * pair]),
        )


def attend_kernel(
    place, slot, q_ref, kv_ref, low_ref, o_ref, lse_ref, ks_ref, kt_ref, query_s, top_s, sum_s, acc_s
):
    per = TILE // 128

    def sort(tile, unused):
        for j in range(per):
            block = kv_ref[slot[tile * per + j]]
            ks_ref[tile, j * 128 : (j + 1) * 128, :] = block
            kt_ref[tile, :, j * 128 : (j + 1) * 128] = block.astype(F32).T.astype(BF16)
        return unused

    lax.fori_loop(0, ks_ref.shape[0], sort, 0)
    apart = lax.broadcasted_iota(jnp.int32, (TILE, 256), 0) - (
        lax.broadcasted_iota(jnp.int32, (TILE, 256), 1) & 127
    )
    count = q_ref.shape[0] // 128
    for b in range(count):
        query = q_ref[b * 128 : (b + 1) * 128, :].astype(F32) * HEAD_DIM**-0.5
        query_s[b] = heads_across(query, 0).astype(BF16)
    top_s[...] = jnp.full(top_s.shape, -1e30, F32)
    sum_s[...] = jnp.zeros(sum_s.shape, F32)
    acc_s[...] = jnp.zeros(acc_s.shape, F32)

    def step(index, unused):
        work = list(turns(place, index, per))
        scores = [
            jnp.where(apart <= own * 128 - tile * TILE, dot(ks_ref[tile], query_s[b]), -1e30)
            for b, tile, own in work
        ]
        for (b, tile, own), score in zip(work, scores):
            top = top_s[b]
            new_top = jnp.maximum(top, jnp.max(score, 0, keepdims=True))
            keep = jnp.exp(top - new_top)
            probs = jnp.exp(score - new_top)
            top_s[b] = new_top
            sum_s[b] = sum_s[b] * keep + jnp.sum(probs, 0, keepdims=True)
            acc_s[b] = acc_s[b] * keep + dot(kt_ref[tile], probs.astype(BF16))
        return unused

    lax.fori_loop(0, ks_ref.shape[0] + 1, step, 0, unroll=3)
    for b in range(count):
        result = acc_s[b][64:] / sum_s[b]
        o_ref[b] = result
        lse_ref[b] = top_s[b] + jnp.log(sum_s[b])
        low_ref[b * 128 : (b + 1) * 128, :] = heads_back(result).astype(BF16)


def attend(place, slot, rq, kv_all):
    count = rq.shape[0] // 128
    tiles = kv_all.shape[0] * 128 // TILE
    return pl.pallas_call(
        attend_kernel,
        grid_spec=pltpu.PrefetchScalarGridSpec(
            num_scalar_prefetch=2,
            grid=(1,),
            in_specs=[
                pl.BlockSpec(rq.shape, lambda i, *_: (0, 0)),
                pl.BlockSpec(kv_all.shape, lambda i, *_: (0, 0, 0)),
            ],
            out_specs=[
                pl.BlockSpec(rq.shape, lambda i, *_: (0, 0)),
                pl.BlockSpec((count, 64, 256), lambda i, *_: (0, 0, 0)),
                pl.BlockSpec((count, 1, 256), lambda i, *_: (0, 0, 0)),
                pl.BlockSpec((tiles, TILE, 128), lambda i, *_: (0, 0, 0)),
                pl.BlockSpec((tiles, 128, TILE), lambda i, *_: (0, 0, 0)),
            ],
            scratch_shapes=[
                pltpu.VMEM((count, 128, 256), BF16),
                pltpu.VMEM((count, 1, 256), F32),
                pltpu.VMEM((count, 1, 256), F32),
                pltpu.VMEM((count, 128, 256), F32),
            ],
        ),
        out_shape=[
            jax.ShapeDtypeStruct(rq.shape, BF16),
            jax.ShapeDtypeStruct((count, 64, 256), F32),
            jax.ShapeDtypeStruct((count, 1, 256), F32),
            jax.ShapeDtypeStruct((tiles, TILE, 128), BF16),
            jax.ShapeDtypeStruct((tiles, 128, TILE), BF16),
        ],
        compiler_params=pltpu.CompilerParams(vmem_limit_bytes=LIMIT),
        cost_estimate=pl.CostEstimate(
            flops=20_000_000_000, bytes_accessed=8_000_000, transcendentals=4_000_000
        ),
        name="attend",
    )(place, slot, rq, kv_all)


def attend_back_kernel(
    place, slot, me, q_ref, full_ref, other_ref, o_ref, lse_ref, ks_ref, kt_ref, cos_ref, sin_ref, wo_ref,
    dq_ref, dkv_ref, da_ref, rest_ref, acc_ref, right_s, under_s, delta_s, dq_s,
):
    per = TILE // 128

    def clear(tile, unused):
        acc_ref[tile] = jnp.zeros((TILE, 128), F32)
        return unused

    lax.fori_loop(0, acc_ref.shape[0], clear, 0)
    few, width = full_ref.shape[1], da_ref.shape[1]
    for b in range(full_ref.shape[0]):
        for ref, side in ((full_ref, me[2]), (other_ref, 1 - me[2])):
            at = pl.ds(pl.multiple_of(b * 2 * few + side * few, few), few)
            da_ref[at, :] = ref[b, :, :width]
            rest_ref[at, :] = ref[b, :, width:]
    apart = lax.broadcasted_iota(jnp.int32, (TILE, 256), 0) - (
        lax.broadcasted_iota(jnp.int32, (TILE, 256), 1) & 127
    )
    count = q_ref.shape[0] // 128
    for b in range(count):
        sl = slice(b * 128, (b + 1) * 128)
        query = heads_across(q_ref[sl, :].astype(F32) * HEAD_DIM**-0.5, 0)
        grad = inner(da_ref[sl, :], wo_ref[...]).astype(BF16)
        grad = heads_across(grad.astype(F32), 64)
        delta_s[b] = jnp.sum(grad[64:] * o_ref[b], 0, keepdims=True)
        right_s[b] = jnp.concatenate([query, grad], 1).astype(BF16)
        under_s[b] = jnp.concatenate([query.T, grad.T], 0).astype(BF16)
    dq_s[...] = jnp.zeros(dq_s.shape, F32)

    def step(index, unused):
        work = list(turns(place, index, per))
        prods = [dot(ks_ref[tile], right_s[b]) for b, tile, own in work]
        sides = []
        for (b, tile, own), prod in zip(work, prods):
            probs = jnp.exp(prod[:, :256] - lse_ref[b])
            probs = jnp.where(apart <= own * 128 - tile * TILE, probs, 0.0)
            dscore = (probs * (prod[:, 256:] - delta_s[b])).astype(BF16)
            sides.append(jnp.concatenate([dscore, probs.astype(BF16)], 1))
        for (b, tile, own), side in zip(work, sides):
            acc_ref[tile] += dot(side, under_s[b])
            dq_s[b] += dot(kt_ref[tile], side[:, :256])
        return unused

    lax.fori_loop(0, ks_ref.shape[0] + 1, step, 0, unroll=3)
    for b in range(count):
        sl = slice(b * 128, (b + 1) * 128)
        dq = heads_back(dq_s[b][:64]) * HEAD_DIM**-0.5
        dq_ref[sl, :] = full_turn(dq, cos_ref[sl, :], -sin_ref[sl, :]).astype(BF16)

    def unsort(tile, unused):
        for j in range(per):
            dkv_ref[slot[tile * per + j]] = acc_ref[tile, j * 128 : (j + 1) * 128, :].astype(BF16)
        return unused

    lax.fori_loop(0, acc_ref.shape[0], unsort, 0)


def attend_back(place, slot, me, rq, full, other, o, lse, ks, kt, cosine, sine, w_out):
    rows = rq.shape[0]
    width = w_out.shape[1]
    blocks = slot.shape[0]
    args = (rq, full, other, o, lse, ks, kt, cosine, sine)
    shapes = [
        jax.ShapeDtypeStruct(rq.shape, BF16),
        jax.ShapeDtypeStruct((blocks, 128, 128), BF16),
        jax.ShapeDtypeStruct((rows, width), BF16),
        jax.ShapeDtypeStruct((rows, 128), BF16),
    ]
    return pl.pallas_call(
        attend_back_kernel,
        grid_spec=pltpu.PrefetchScalarGridSpec(
            num_scalar_prefetch=3,
            grid=(1,),
            in_specs=[whole(a) for a in args]
            + [pl.BlockSpec((rq.shape[1], width), lambda i, place, slot, me: (me[0], 0))],
            out_specs=[whole(a) for a in shapes],
            scratch_shapes=[
                pltpu.VMEM(ks.shape, F32),
                pltpu.VMEM((rows // 128, 128, 512), BF16),
                pltpu.VMEM((rows // 128, 512, 128), BF16),
                pltpu.VMEM((rows // 128, 1, 256), F32),
                pltpu.VMEM((rows // 128, 128, 256), F32),
            ],
        ),
        out_shape=shapes,
        compiler_params=pltpu.CompilerParams(vmem_limit_bytes=LIMIT),
        cost_estimate=pl.CostEstimate(
            flops=30_000_000_000, bytes_accessed=8_000_000, transcendentals=4_000_000
        ),
        name="attend_back",
    )(place, slot, me, *args, w_out)


def whole(a):
    rank = len(a.shape)
    return pl.BlockSpec(a.shape, lambda i, *_: (0,) * rank, pipeline_mode=pl.Buffered(1))


def experts_kernel(
    me, o_ref, p_ref, x_ref, dy_ref, routes_ref, wo0, wo1, wo2, wo3, gain_ref, wr_ref,
    wg_ref, wu_ref, wd_ref,
    x2_ref, h2_ref, mix_ref, keep_ref, give_ref, mkeep_ref, mgive_ref, grad_ref,
    dh2_acc, moe_acc, dmix_acc, mix_s,
):
    step = pl.program_id(0)
    xh, core, first = me[1], me[2], me[3]
    rows = x_ref.shape[0]
    lane = lax.broadcasted_iota(jnp.int32, (rows, 128), 1)

    @pl.when(step == 0)
    def _():
        def heads(ref, side):
            return jnp.concatenate([ref[side], ref[2 + side]], 1)

        near = dot(heads(o_ref, xh), wo0[...]) + dot(heads(p_ref, xh), wo1[...])
        far = dot(heads(o_ref, 1 - xh), wo2[...]) + dot(heads(p_ref, 1 - xh), wo3[...])
        x2 = x_ref[...].astype(F32) + (near + far)
        few = rows // 8
        for j in range(8):

            @pl.when(me[4] == j)
            def _(j=j):
                x2_ref[...] = x2[j * few : (j + 1) * few]

        h2 = rms(x2, gain_ref[...])[0].astype(BF16)
        h2_ref[...] = h2
        logits = dot(h2, wr_ref[...])
        routes = routes_ref[...]
        used = lane == routes[:, 0:1]
        for k in range(1, routes.shape[1]):
            used = jnp.logical_or(used, lane == routes[:, k : k + 1])
        top = jnp.max(jnp.where(used, logits, -jnp.inf), 1, keepdims=True)
        expd = jnp.where(used, jnp.exp(logits - top), 0.0)
        mix_s[...] = expd / jnp.sum(expd, 1, keepdims=True)
        mix_ref[...] = mix_s[pl.ds(pl.multiple_of(me[4] * few, few), few), :]
        dh2_acc[...] = jnp.zeros_like(dh2_acc)
        moe_acc[...] = jnp.zeros_like(moe_acc)
        dmix_acc[...] = jnp.zeros_like(dmix_acc)

    here = lane == first + step
    gate = jnp.sum(jnp.where(here, mix_s[...], 0.0), 1, keepdims=True)
    h2 = h2_ref[...]
    dy = dy_ref[...].astype(F32)
    ga = dot(h2, wg_ref[0])
    up = dot(h2, wu_ref[0])
    sig = jax.nn.sigmoid(ga)
    act = ga * sig
    hid = (act * up).astype(BF16)
    eo = dot(hid, wd_ref[0])
    moe_acc[...] += gate * eo
    dmix_acc[...] += jnp.where(here, jnp.sum(dy * eo, 1, keepdims=True), 0.0)
    deo = (gate * dy).astype(BF16)
    dhid = inner(deo, wd_ref[0])
    dga = (dhid * up * (sig * (1.0 + ga * (1.0 - sig)))).astype(BF16)
    dup = (dhid * act).astype(BF16)
    dh2_acc[...] += inner(dga, wg_ref[0]) + inner(dup, wu_ref[0])
    groups = grad_ref.shape[0]
    across = grad_ref.shape[2] * 2 // 3
    width = h2.shape[1]
    grad_ref[:, 0, :across, :512] = outer(h2, dga).astype(BF16).reshape(groups, across, 512)
    grad_ref[:, 0, :across, 512:] = outer(h2, dup).astype(BF16).reshape(groups, across, 512)
    grad_ref[:, 0, across:, :] = outer(hid, deo).astype(BF16).reshape(groups, across // 2, width)

    @pl.when(step == pl.num_programs(0) - 1)
    def _():
        few = rows // 8
        for j in range(4):
            for side, out, mout in ((core, keep_ref, mkeep_ref), (1 - core, give_ref, mgive_ref)):
                at = pl.ds(pl.multiple_of((j * 2 + side) * few, few), few)
                out[j, :, :width] = dh2_acc[at, :].astype(BF16)
                out[j, :, width:] = dmix_acc[at, :].astype(BF16)
                mout[j] = moe_acc[at, :].astype(BF16)


def experts(me, o_mine, o_other, x_pair, dy_pair, routes, wo, gain, router, wg, wu, wd, groups):
    rows, width = x_pair.shape
    few = rows // 8
    local = wg.shape[0] // 2
    ff = wg.shape[2]
    args = (o_mine, o_other, x_pair, dy_pair, routes, *wo, gain, router)
    shapes = [
        jax.ShapeDtypeStruct((few, width), F32),
        jax.ShapeDtypeStruct((rows, width), BF16),
        jax.ShapeDtypeStruct((few, 128), F32),
        jax.ShapeDtypeStruct((4, few, width + 128), BF16),
        jax.ShapeDtypeStruct((4, few, width + 128), BF16),
        jax.ShapeDtypeStruct((4, few, width), BF16),
        jax.ShapeDtypeStruct((4, few, width), BF16),
    ]
    pick = lambda i, me: (me[0] * local + i, 0, 0)
    across = width // groups
    return pl.pallas_call(
        experts_kernel,
        grid_spec=pltpu.PrefetchScalarGridSpec(
            num_scalar_prefetch=1,
            grid=(local,),
            in_specs=[whole(a) for a in args]
            + [
                pl.BlockSpec((1, width, ff), pick),
                pl.BlockSpec((1, width, ff), pick),
                pl.BlockSpec((1, ff, width), pick),
            ],
            out_specs=[whole(a) for a in shapes]
            + [pl.BlockSpec((groups, 1, across * 3 // 2, width), lambda i, me: (0, i, 0, 0))],
            scratch_shapes=[
                pltpu.VMEM((rows, width), F32),
                pltpu.VMEM((rows, width), F32),
                pltpu.VMEM((rows, 128), F32),
                pltpu.VMEM((rows, 128), F32),
            ],
        ),
        out_shape=shapes
        + [jax.ShapeDtypeStruct((groups, local, across * 3 // 2, width), BF16)],
        compiler_params=pltpu.CompilerParams(vmem_limit_bytes=EXPERT_LIMIT),
        cost_estimate=pl.CostEstimate(
            flops=15_000_000_000, bytes_accessed=20_000_000, transcendentals=1_000_000
        ),
        name="experts",
    )(me, *args, wg, wu, wd)


def start_kernel(me, x_ref, gain_ref, wq_ref, wk_ref, wv_ref, cos_ref, sin_ref, keep_ref, give_ref):
    h1 = rms(x_ref[...].astype(F32), gain_ref[...])[0].astype(BF16)
    cosine, sine = cos_ref[...], sin_ref[...]
    query = full_turn(dot(h1, wq_ref[...]), cosine, sine)
    key = full_turn(dot(h1, wk_ref[...]), cosine, sine)
    value = dot(h1, wv_ref[...])
    left = lax.broadcasted_iota(jnp.int32, key.shape, 1) < 64
    halves = [
        jnp.concatenate([query[:, :128], jnp.where(left, key, pltpu.roll(value, 64, 1))], 1),
        jnp.concatenate([query[:, 128:], jnp.where(left, pltpu.roll(key, 64, 1), value)], 1),
    ]
    low = me[0] == 0
    keep_ref[...] = jnp.where(low, halves[0], halves[1]).astype(BF16)
    give_ref[...] = jnp.where(low, halves[1], halves[0]).astype(BF16)


def start(me, tokens, gain, wq, wk, wv, cosine, sine):
    args = (tokens, gain, wq, wk, wv, cosine, sine)
    shapes = [jax.ShapeDtypeStruct((tokens.shape[0], 256), BF16)] * 2
    return pl.pallas_call(
        start_kernel,
        grid_spec=pltpu.PrefetchScalarGridSpec(
            num_scalar_prefetch=1,
            grid=(1,),
            in_specs=[whole(a) for a in args],
            out_specs=[whole(a) for a in shapes],
        ),
        out_shape=shapes,
        compiler_params=pltpu.CompilerParams(vmem_limit_bytes=60 * 1024 * 1024),
        name="start",
    )(me, *args)


def middle_kernel(me, part_ref, x2_ref, mix_ref, dy_ref, gain_ref, wr_ref, out_ref):
    part = part_ref[0].astype(F32)
    for j in range(1, part_ref.shape[0]):
        part = part + part_ref[j].astype(F32)
    width = x2_ref.shape[1]
    mix, dmix = mix_ref[...], part[:, width:]
    dlogits = (mix * (dmix - jnp.sum(mix * dmix, 1, keepdims=True))).astype(BF16)
    dh2 = part[:, :width] + inner(dlogits, wr_ref[...])
    x2 = x2_ref[...]
    factor = lax.rsqrt(jnp.mean(x2 * x2, -1, keepdims=True) + EPS)
    scaled = dh2 * gain_ref[...]
    dx2 = dy_ref[...].astype(F32) + (
        factor * scaled - x2 * factor**3 * jnp.mean(scaled * x2, -1, keepdims=True)
    )
    gain = jnp.sum(dh2 * x2 * factor, 0, keepdims=True).astype(BF16).astype(F32)
    rows = x2.shape[0]
    per = width // rows
    at = lax.broadcasted_iota(jnp.int32, (rows, width), 1)
    spread = jnp.where(at // per == lax.broadcasted_iota(jnp.int32, (rows, width), 0), gain, 0.0)
    lane = lax.broadcasted_iota(jnp.int32, (width, 128), 1)
    place = lane == lax.broadcasted_iota(jnp.int32, (width, 128), 0) % per + 16
    extra = dot(spread.astype(BF16), place.astype(F32).astype(BF16)) + dlogits.astype(F32)
    for j in range(out_ref.shape[0]):
        out_ref[j, :, :width] = dx2.astype(BF16)
        out_ref[j, :, width:] = extra.astype(BF16)


def middle(me, part, x2, mix, dy, gain, router):
    few = part.shape[1]
    width = x2.shape[1]
    mine = lambda i, me: (me[4], 0)
    shape = jax.ShapeDtypeStruct(part.shape, BF16)
    return pl.pallas_call(
        middle_kernel,
        grid_spec=pltpu.PrefetchScalarGridSpec(
            num_scalar_prefetch=1,
            grid=(1,),
            in_specs=[
                whole(part),
                whole(x2),
                whole(mix),
                pl.BlockSpec((few, width), mine),
                whole(gain),
                whole(router),
            ],
            out_specs=whole(shape),
        ),
        out_shape=shape,
        compiler_params=pltpu.CompilerParams(vmem_limit_bytes=LIMIT),
        name="middle",
    )(me, part, x2, mix, dy, gain, router)


def collect_kernel(part_ref, cos_ref, sin_ref, out_ref):
    total = part_ref[0].astype(F32)
    for j in range(1, part_ref.shape[0]):
        total = total + part_ref[j].astype(F32)
    turned = full_turn(total, cos_ref[...], -sin_ref[...])
    left = lax.broadcasted_iota(jnp.int32, total.shape, 1) < 64
    out_ref[...] = jnp.where(left, turned, total).astype(BF16)


def collect(part, cosine, sine):
    shape = jax.ShapeDtypeStruct(part.shape[1:], BF16)
    args = (part, cosine, sine)
    return pl.pallas_call(
        collect_kernel,
        grid=(1,),
        in_specs=[whole(a) for a in args],
        out_specs=whole(shape),
        out_shape=shape,
        compiler_params=pltpu.CompilerParams(vmem_limit_bytes=LIMIT),
        name="collect",
    )(*args)


def finish_kernel(
    me, m_ref, o_ref, w0, w1, w2, w3, x_ref, gain_ref, da_ref,
    early_ref, gkv_ref, rest_ref, out_ref, small_ref,
):
    xh = me[1]

    def back(ref, side, w):
        one, two = ref[side], ref[2 + side]
        hq = one.shape[1] // 2
        left = lax.broadcasted_iota(jnp.int32, (one.shape[0], hq), 1) < 64
        low, high = one[:, hq:].astype(F32), two[:, hq:].astype(F32)
        keys = jnp.where(left, low, pltpu.roll(high, 64, 1)).astype(BF16)
        values = jnp.where(left, pltpu.roll(low, 64, 1), high).astype(BF16)
        return inner(jnp.concatenate([one[:, :hq], two[:, :hq], keys, values], 1), w[...])

    near = back(m_ref, xh, w0) + back(o_ref, xh, w1)
    far = back(m_ref, 1 - xh, w2) + back(o_ref, 1 - xh, w3)
    dh1 = near + far
    x = x_ref[...].astype(F32)
    factor = lax.rsqrt(jnp.mean(x * x, -1, keepdims=True) + EPS)
    scaled = dh1 * gain_ref[...]
    out_ref[...] = (
        da_ref[...].astype(F32)
        + factor * scaled
        - x * factor**3 * jnp.mean(scaled * x, -1, keepdims=True)
    ).astype(BF16)
    gain = jnp.sum(dh1 * x * factor, 0, keepdims=True)
    width = gain.shape[1]
    column = jnp.broadcast_to(gain, (128, width)).T
    lane = lax.broadcasted_iota(jnp.int32, (width, 128), 1)
    mark = rest_ref.shape[1] - 1
    small_ref[:, :256] = early_ref[...]
    small_ref[:, 256:384] = gkv_ref[...]
    small_ref[:, 384:] = jnp.where(lane == mark, column, rest_ref[...].astype(F32)).astype(BF16)


def finish(me, mine, other, ws, tokens, gain, da, early, gkv, rest):
    rows, width = tokens.shape
    args = (mine, other, *ws, tokens, gain)
    shapes = [
        jax.ShapeDtypeStruct((rows, width), BF16),
        jax.ShapeDtypeStruct((width, 512), BF16),
    ]
    return pl.pallas_call(
        finish_kernel,
        grid_spec=pltpu.PrefetchScalarGridSpec(
            num_scalar_prefetch=1,
            grid=(1,),
            in_specs=[whole(a) for a in args]
            + [pl.BlockSpec((rows, width), lambda i, me: (me[0], 0))]
            + [whole(a) for a in (early, gkv, rest)],
            out_specs=[whole(a) for a in shapes],
        ),
        out_shape=shapes,
        compiler_params=pltpu.CompilerParams(vmem_limit_bytes=LIMIT),
        name="finish",
    )(me, *args, da, early, gkv, rest)


def unpack_kernel(
    me, part_ref, keep_ref, got_ref, own_ref, near_ref, far_ref, last_ref,
    q_ref, k_ref, v_ref, o_ref, r_ref, nm_ref, na_ref, gate_ref, up_ref, down_ref, out_ref,
):
    local, few = keep_ref.shape[0], own_ref.shape[0]
    for ref, side in ((keep_ref, me[0]), (got_ref, 1 - me[0])):
        for e in range(local):
            gate_ref[side * local + e] = ref[e, : gate_ref.shape[1], : gate_ref.shape[2]].astype(F32)
            up_ref[side * local + e] = ref[e, : gate_ref.shape[1], gate_ref.shape[2] :].astype(F32)
            down_ref[side * local + e] = ref[e, gate_ref.shape[1] :, :].astype(F32)
    for ref, xh, core in (
        (own_ref, me[1], me[2]),
        (near_ref, me[1], 1 - me[2]),
        (far_ref, 1 - me[1], me[2]),
        (last_ref, 1 - me[1], 1 - me[2]),
    ):
        out_ref[pl.ds(pl.multiple_of((xh * 2 + core) * few, few), few), :] = ref[...]
    groups = part_ref.shape[0] // 2
    sums = []
    for side in (0, 1):
        total = part_ref[side].astype(F32)
        for j in range(1, groups):
            total = total + part_ref[2 * j + side].astype(F32)
        sums.append(total)
    one, two = sums
    q_ref[...] = jnp.concatenate([one[:, :128], two[:, :128]], 1)
    o_ref[...] = jnp.concatenate([one[:, 128:256], two[:, 128:256]], 1)
    left = lax.broadcasted_iota(jnp.int32, (one.shape[0], 128), 1) < 64
    low, high = one[:, 256:384], two[:, 256:384]
    k_ref[...] = jnp.where(left, low, pltpu.roll(high, 64, 1))
    v_ref[...] = jnp.where(left, pltpu.roll(low, 64, 1), high)
    rest = one[:, 384:] + two[:, 384:]
    rest = jnp.concatenate([rest, jnp.zeros((128 - rest.shape[0], 128), F32)], 0).T
    rows = q_ref.shape[0]
    count = r_ref.shape[0]
    r_ref[...] = rest[:count, :rows]
    nm_ref[...] = rest[count : count + 1, :rows]
    na_ref[...] = rest[127:, :rows]


def unpack(me, part, keep, got, outs, experts_all):
    rows = part.shape[1]
    local, width = keep.shape[0], keep.shape[2]
    args = (part, keep, got, *outs)
    shapes = [
        jax.ShapeDtypeStruct(n, F32)
        for n in (
            (rows, 256), (rows, 128), (rows, 128), (rows, 256), (experts_all, rows), (1, rows), (1, rows),
            (2 * local, rows, width // 2), (2 * local, rows, width // 2), (2 * local, rows // 2, width),
        )
    ] + [jax.ShapeDtypeStruct((4 * outs[0].shape[0], width), BF16)]
    return pl.pallas_call(
        unpack_kernel,
        grid_spec=pltpu.PrefetchScalarGridSpec(
            num_scalar_prefetch=1,
            grid=(1,),
            in_specs=[whole(a) for a in args],
            out_specs=[whole(a) for a in shapes],
        ),
        out_shape=shapes,
        compiler_params=pltpu.CompilerParams(vmem_limit_bytes=LIMIT),
        name="unpack",
    )(me, *args)


def on_device(
    tokens,
    cotangent,
    pairing,
    routes,
    norm_attn,
    w_query,
    w_key,
    w_value,
    w_out,
    norm_moe,
    w_router,
    w_gate,
    w_up,
    w_down,
):
    zy = lax.axis_index(ZY)
    xl = lax.axis_index("xl")
    wa = lax.axis_index(WA)
    rows, width = tokens.shape
    block = rows // 2
    both = 2 * rows
    count_ctx = pairing.shape[0]
    blocks = 2 * count_ctx
    groups = count_ctx // 2
    hq = w_query.shape[1] // 2
    hk = w_key.shape[1] // 2
    hall = hq + 2 * hk

    xh = lax.axis_index("xh")
    core = lax.axis_index("c")
    first = wa * w_gate.shape[0] + xl * (w_gate.shape[0] // 2)
    me = jnp.stack([xl, xh, core, first, xl * 4 + wa]).astype(jnp.int32)

    pair = lax.dynamic_slice_in_dim(pairing, zy * 2, 2)
    starts = jnp.stack([pair, blocks - 1 - pair], 1).reshape(4) * block
    qpos = (starts[:, None] + jnp.arange(block, dtype=jnp.int32)[None, :]).reshape(both)

    cos2, sin2 = lane_angles(qpos)
    own = lambda a: lax.dynamic_slice_in_dim(a, xl * rows, rows, 0)
    keep, give = start(
        me, tokens, norm_attn[None], w_query, w_key, w_value, own(cos2), own(sin2)
    )
    got = lax.ppermute(give, "xl", SWAP)
    low = xl == 0
    qkv = jnp.concatenate([jnp.where(low, keep, got), jnp.where(low, got, keep)], 0)
    rq = qkv[:, :hq]
    kv_mine = qkv[:, hq:]

    kv_all = lax.all_to_all(
        jnp.broadcast_to(kv_mine[None], (groups,) + kv_mine.shape), ZY, 0, 0, tiled=False
    ).reshape(blocks, block, 2 * hk)

    def ring_weights(w):
        near = lax.ppermute(w, "c", SWAP)
        far = lax.ppermute(w, "xh", SWAP)
        return w, near, far, lax.ppermute(far, "c", SWAP)

    w_outs = ring_weights(w_out)

    def ring_parts(w):
        return w, lax.ppermute(w, "c", SWAP), lax.ppermute(w, "xh", SWAP), lax.ppermute(
            w, WA, [(0, 3), (3, 0), (1, 2), (2, 1)]
        )

    x_pair = swap_x(tokens)
    routes_pair = swap_x(routes.astype(F32)).astype(jnp.int32)
    h1 = rms(x_pair.astype(F32), norm_attn)[0].astype(BF16)
    kv_all, x_pair, routes_pair, h1, cotangent = lax.optimization_barrier(
        (kv_all, x_pair, routes_pair, h1, cotangent)
    )
    dy_other = lax.ppermute(cotangent, "xl", SWAP)

    ranks = jnp.arange(count_ctx, dtype=jnp.int32)
    inverse = jnp.sum(jnp.where(pairing[None, :] == ranks[:, None], ranks[None, :], 0), 1)
    slot = jnp.concatenate([inverse * 2, inverse[::-1] * 2 + 1])
    place = starts // block
    attn_low, attn, lse, ks, kt = attend(place, slot, rq, kv_all)
    attn_low, dy_other, w_outs = lax.optimization_barrier((attn_low, dy_other, w_outs))
    dy_pair = in_pair(cotangent, dy_other)

    o_mine = lax.all_to_all(
        jnp.broadcast_to(attn_low[None], (4,) + attn_low.shape), CHIPS, 0, 0, tiled=False
    )
    w_in = jnp.concatenate([w_query, w_key, w_value], 1)
    o_mine, w_in, dy_pair = lax.optimization_barrier((o_mine, w_in, dy_pair))
    o_other = lax.ppermute(o_mine, "c", SWAP)
    experts_all = w_router.shape[1]
    router = jnp.pad(w_router, ((0, 0), (0, 128 - experts_all)))
    x2_rows, h2, mix_rows, keep, give, mkeep, mgive, grads = experts(
        me, o_mine, o_other, x_pair, dy_pair, routes_pair, w_outs, norm_moe[None], router,
        w_gate, w_up, w_down, groups,
    )

    def add(one, two):
        return (one.astype(F32) + two.astype(F32)).astype(BF16)

    part = add(keep, lax.ppermute(give, "c", SWAP))
    part = lax.all_to_all(part, CHIPS, 0, 0, tiled=False)
    grads = lax.psum_scatter(grads, "z", scatter_dimension=0, tiled=True)
    payload = middle(me, part, x2_rows, mix_rows, dy_pair, norm_moe[None], router)
    full = lax.all_to_all(payload, CHIPS, 0, 0, tiled=False)
    other = lax.ppermute(full, "c", SWAP)

    w_in, _ = lax.optimization_barrier((w_in, full))
    w_ins = ring_weights(w_in)
    dq, grad_kv, da, rest_pair = attend_back(
        place, slot, me, rq, full, other, attn, lse, ks, kt, cos2, sin2, w_out
    )
    mkeep, mgot, _ = lax.optimization_barrier(
        (mkeep, lax.ppermute(mgive, "c", SWAP), grad_kv)
    )
    moe = add(mkeep, mgot).reshape(2, 2, both // 8, width)
    at = lambda a, b: lax.dynamic_index_in_dim(
        lax.dynamic_index_in_dim(moe, a, 0, False), b, 0, False
    )
    few = both // 8
    moe_rows = (
        at(xl, xh).astype(F32)
        + lax.ppermute(at(1 - xl, xh), "xl", SWAP).astype(F32)
        + lax.ppermute(at(xl, 1 - xh), "xh", SWAP).astype(F32)
        + lax.ppermute(at(1 - xl, 1 - xh), CHIPS, [(0, 3), (3, 0), (1, 2), (2, 1)]).astype(F32)
    )
    out_rows = (x2_rows + moe_rows).astype(BF16)
    gnm_all = rest_pair[:, experts_all : experts_all + width // few].astype(F32)
    gnm_own = jnp.sum(own(gnm_all).reshape(4, few, width // few), 0).reshape(width)
    grad_kv = lax.all_to_all(
        grad_kv.reshape(groups, both, 2 * hk), ZY, 0, 0, tiled=False
    )
    h2_own = own(h2)
    rest = jnp.concatenate(
        [outer(h2_own, own(rest_pair)[:, :experts_all]), gnm_own[:, None]], 1
    ).astype(BF16)
    rest = jnp.pad(rest, ((0, 0), (0, 128 - rest.shape[1])))
    early = jnp.concatenate([outer(h1, dq), outer(da, attn_low)], 1).astype(BF16)
    outs = ring_parts(out_rows)
    grad_kv, rest, early, outs, w_ins, grads = lax.optimization_barrier(
        (grad_kv, rest, early, outs, w_ins, grads)
    )
    grads = lax.psum_scatter(grads, "y", scatter_dimension=0, tiled=True)[0]
    dkv = collect(grad_kv, cos2, sin2)

    def to_rows(piece):
        n = piece.shape[1]
        mine = lax.all_to_all(
            jnp.broadcast_to(piece.reshape(2, 1, rows, n), (2, 2, rows, n)).reshape(4, rows, n),
            CHIPS, 0, 0, tiled=False,
        )
        return mine, lax.ppermute(mine, "c", SWAP)

    d_mine, d_other = to_rows(jnp.concatenate([dq, dkv], 1))
    gkv = outer(h1, dkv).astype(BF16)
    grad_tokens, small = finish(
        me, d_mine, d_other, w_ins, tokens, norm_attn[None], da,
        early, gkv, rest,
    )

    local = grads.shape[0]
    nrow = width // groups // 2
    by_dest = jnp.concatenate(
        [
            grads[:, : 2 * nrow].reshape(local, 2, nrow, width),
            grads[:, 2 * nrow :].reshape(local, 2, nrow // 2, width),
        ],
        2,
    ).transpose(1, 0, 2, 3)
    by_dest, _ = lax.optimization_barrier((by_dest, small))
    keep_w = lax.dynamic_index_in_dim(by_dest, xl, 0, False)
    got_w = lax.ppermute(lax.dynamic_index_in_dim(by_dest, 1 - xl, 0, False), "xl", SWAP)

    small = lax.all_to_all(small.reshape(count_ctx, -1, small.shape[1]), CTX, 0, 0, tiled=False)
    (
        grad_query, grad_key, grad_value, grad_out, grad_router, gnm, gna, grad_gate, grad_up,
        grad_down, output,
    ) = unpack(me, small, keep_w, got_w, outs, experts_all)
    grad_out, grad_router = grad_out.T, grad_router.T
    grad_norm_moe, grad_norm_attn = gnm.reshape(-1), gna.reshape(-1)
    return (
        output,
        grad_tokens,
        grad_norm_attn,
        grad_query,
        grad_key,
        grad_value,
        grad_out,
        grad_norm_moe,
        grad_router,
        grad_gate,
        grad_up,
        grad_down,
    )


def solution(mesh):
    fine = Mesh(mesh.devices.reshape(4, 4, 2, 2, 2), ("z", "y", "xl", "xh", "c"))
    return jax.shard_map(
        on_device,
        mesh=fine,
        in_specs=(
            P(CTX, None),
            P(CTX, None),
            P(),
            P(CTX, None),
            P(),
            P(None, WA),
            P(None, WA),
            P(None, WA),
            P(WA, None),
            P(),
            P(),
            P(WA, None, None),
            P(WA, None, None),
            P(WA, None, None),
        ),
        out_specs=(
            P(CTX, None),
            P(CTX, None),
            P(CTX),
            P(CTX, WA),
            P(CTX, WA),
            P(CTX, WA),
            P(WA, CTX),
            P(CTX),
            P(CTX, None),
            P(WA, CTX, None),
            P(WA, CTX, None),
            P(WA, CTX, None),
        ),
        check_vma=False,
    )
```

```python
import jax
import jax.numpy as jnp
from jax import lax
from jax.experimental import pallas as pl
from jax.experimental.pallas import tpu as pltpu
from jax.sharding import Mesh
from jax.sharding import PartitionSpec as P

HEAD_DIM = 64
EPS = 1e-05
THETA = 10000.0
CTX = ("z", "y", "xl")
WA = ("xh", "c")
ZY = ("z", "y")
CHIPS = ("xl", "xh")
BF16 = jnp.bfloat16
F32 = jnp.float32
SWAP = [(0, 1), (1, 0)]


def dot(left, right):
    return jnp.dot(left, right, preferred_element_type=F32)


def outer(left, right):
    return lax.dot_general(left, right, (((0,), (0,)), ((), ())), preferred_element_type=F32)


def inner(left, right):
    return lax.dot_general(left, right, (((1,), (1,)), ((), ())), preferred_element_type=F32)


def rms(values, gain):
    factor = lax.rsqrt(jnp.mean(values * values, -1, keepdims=True) + EPS)
    return values * factor * gain, factor


def swap_x(mine):
    return in_pair(mine, lax.ppermute(mine, "xl", SWAP))


def in_pair(mine, other):
    low = lax.axis_index("xl") == 0
    return jnp.concatenate([jnp.where(low, mine, other), jnp.where(low, other, mine)], 0)


TILE = 1024
LIMIT = 40 * 1024 * 1024
EXPERT_LIMIT = 56 * 1024 * 1024


def full_turn(flat, cosine, sine):
    rows, width = flat.shape
    lane = lax.broadcasted_iota(jnp.int32, (rows, 128), 1)
    first = (lane & 63) < 32
    parts = []
    for n in range(width // 128):
        piece = flat[:, n * 128 : (n + 1) * 128]
        other = jnp.where(first, pltpu.roll(piece, 96, 1), pltpu.roll(piece, 32, 1))
        parts.append(piece * cosine + other * sine)
    return parts[0] if len(parts) == 1 else jnp.concatenate(parts, 1)


def lane_angles(pos):
    lane = jnp.arange(128, dtype=jnp.int32)
    freq = THETA ** (-((lane % 32).astype(F32) * 2.0 / HEAD_DIM))
    angle = pos.astype(F32)[:, None] * freq[None, :]
    sign = jnp.where(lane % 64 < 32, -1.0, 1.0)
    return jnp.cos(angle), jnp.sin(angle) * sign[None, :]


def heads_across(block, low):
    turned = block.T
    both = jnp.concatenate([turned[:64], turned[64:]], 1)
    zero = jnp.zeros_like(both)
    return jnp.concatenate([both, zero] if low == 0 else [zero, both], 0)


def heads_back(both):
    return jnp.concatenate([both[:, :128], both[:, 128:]], 0).T


def turns(place, step, per):
    for pair in (0, 1):
        late = place[2 * pair + 1]
        count = late // per + 1
        first = step < count
        yield (
            jnp.where(first, 2 * pair + 1, 2 * pair),
            jnp.where(first, step, step - count),
            jnp.where(first, late, place[2 * pair]),
        )


def attend_kernel(
    place, slot, q_ref, kv_ref, low_ref, o_ref, lse_ref, ks_ref, kt_ref, query_s, top_s, sum_s, acc_s
):
    per = TILE // 128

    def sort(tile, unused):
        for j in range(per):
            block = kv_ref[slot[tile * per + j]]
            ks_ref[tile, j * 128 : (j + 1) * 128, :] = block
            kt_ref[tile, :, j * 128 : (j + 1) * 128] = block.astype(F32).T.astype(BF16)
        return unused

    lax.fori_loop(0, ks_ref.shape[0], sort, 0)
    apart = lax.broadcasted_iota(jnp.int32, (TILE, 256), 0) - (
        lax.broadcasted_iota(jnp.int32, (TILE, 256), 1) & 127
    )
    count = q_ref.shape[0] // 128
    for b in range(count):
        query = q_ref[b * 128 : (b + 1) * 128, :].astype(F32) * HEAD_DIM**-0.5
        query_s[b] = heads_across(query, 0).astype(BF16)
    top_s[...] = jnp.full(top_s.shape, -1e30, F32)
    sum_s[...] = jnp.zeros(sum_s.shape, F32)
    acc_s[...] = jnp.zeros(acc_s.shape, F32)

    def step(index, unused):
        work = list(turns(place, index, per))
        scores = [
            jnp.where(apart <= own * 128 - tile * TILE, dot(ks_ref[tile], query_s[b]), -1e30)
            for b, tile, own in work
        ]
        for (b, tile, own), score in zip(work, scores):
            top = top_s[b]
            new_top = jnp.maximum(top, jnp.max(score, 0, keepdims=True))
            keep = jnp.exp(top - new_top)
            probs = jnp.exp(score - new_top)
            top_s[b] = new_top
            sum_s[b] = sum_s[b] * keep + jnp.sum(probs, 0, keepdims=True)
            acc_s[b] = acc_s[b] * keep + dot(kt_ref[tile], probs.astype(BF16))
        return unused

    lax.fori_loop(0, ks_ref.shape[0] + 1, step, 0, unroll=9)
    for b in range(count):
        result = acc_s[b][64:] / sum_s[b]
        o_ref[b] = result
        lse_ref[b] = top_s[b] + jnp.log(sum_s[b])
        low_ref[b * 128 : (b + 1) * 128, :] = heads_back(result).astype(BF16)


def attend(place, slot, rq, kv_all):
    count = rq.shape[0] // 128
    tiles = kv_all.shape[0] * 128 // TILE
    return pl.pallas_call(
        attend_kernel,
        grid_spec=pltpu.PrefetchScalarGridSpec(
            num_scalar_prefetch=2,
            grid=(1,),
            in_specs=[
                pl.BlockSpec(rq.shape, lambda i, *_: (0, 0)),
                pl.BlockSpec(kv_all.shape, lambda i, *_: (0, 0, 0)),
            ],
            out_specs=[
                pl.BlockSpec(rq.shape, lambda i, *_: (0, 0)),
                pl.BlockSpec((count, 64, 256), lambda i, *_: (0, 0, 0)),
                pl.BlockSpec((count, 1, 256), lambda i, *_: (0, 0, 0)),
                pl.BlockSpec((tiles, TILE, 128), lambda i, *_: (0, 0, 0)),
                pl.BlockSpec((tiles, 128, TILE), lambda i, *_: (0, 0, 0)),
            ],
            scratch_shapes=[
                pltpu.VMEM((count, 128, 256), BF16),
                pltpu.VMEM((count, 1, 256), F32),
                pltpu.VMEM((count, 1, 256), F32),
                pltpu.VMEM((count, 128, 256), F32),
            ],
        ),
        out_shape=[
            jax.ShapeDtypeStruct(rq.shape, BF16),
            jax.ShapeDtypeStruct((count, 64, 256), F32),
            jax.ShapeDtypeStruct((count, 1, 256), F32),
            jax.ShapeDtypeStruct((tiles, TILE, 128), BF16),
            jax.ShapeDtypeStruct((tiles, 128, TILE), BF16),
        ],
        compiler_params=pltpu.CompilerParams(vmem_limit_bytes=LIMIT),
        cost_estimate=pl.CostEstimate(
            flops=20_000_000_000, bytes_accessed=8_000_000, transcendentals=4_000_000
        ),
        name="attend",
    )(place, slot, rq, kv_all)


def attend_back_kernel(
    place, slot, me, q_ref, full_ref, other_ref, o_ref, lse_ref, ks_ref, kt_ref, cos_ref, sin_ref, wo_ref,
    dq_ref, dkv_ref, da_ref, rest_ref, acc_ref, right_s, under_s, delta_s, dq_s,
):
    per = TILE // 128

    def clear(tile, unused):
        acc_ref[tile] = jnp.zeros((TILE, 128), F32)
        return unused

    lax.fori_loop(0, acc_ref.shape[0], clear, 0)
    few, width = full_ref.shape[1], da_ref.shape[1]
    for b in range(full_ref.shape[0]):
        for ref, side in ((full_ref, me[2]), (other_ref, 1 - me[2])):
            at = pl.ds(pl.multiple_of(b * 2 * few + side * few, few), few)
            da_ref[at, :] = ref[b, :, :width]
            rest_ref[at, :] = ref[b, :, width:]
    apart = lax.broadcasted_iota(jnp.int32, (TILE, 256), 0) - (
        lax.broadcasted_iota(jnp.int32, (TILE, 256), 1) & 127
    )
    count = q_ref.shape[0] // 128
    for b in range(count):
        sl = slice(b * 128, (b + 1) * 128)
        query = heads_across(q_ref[sl, :].astype(F32) * HEAD_DIM**-0.5, 0)
        grad = inner(da_ref[sl, :], wo_ref[...]).astype(BF16)
        grad = heads_across(grad.astype(F32), 64)
        delta_s[b] = jnp.sum(grad[64:] * o_ref[b], 0, keepdims=True)
        right_s[b] = jnp.concatenate([query, grad], 1).astype(BF16)
        under_s[b] = jnp.concatenate([query.T, grad.T], 0).astype(BF16)
    dq_s[...] = jnp.zeros(dq_s.shape, F32)

    def step(index, unused):
        work = list(turns(place, index, per))
        prods = [dot(ks_ref[tile], right_s[b]) for b, tile, own in work]
        sides = []
        for (b, tile, own), prod in zip(work, prods):
            probs = jnp.exp(prod[:, :256] - lse_ref[b])
            probs = jnp.where(apart <= own * 128 - tile * TILE, probs, 0.0)
            dscore = (probs * (prod[:, 256:] - delta_s[b])).astype(BF16)
            sides.append(jnp.concatenate([dscore, probs.astype(BF16)], 1))
        for (b, tile, own), side in zip(work, sides):
            acc_ref[tile] += dot(side, under_s[b])
            dq_s[b] += dot(kt_ref[tile], side[:, :256])
        return unused

    lax.fori_loop(0, ks_ref.shape[0] + 1, step, 0, unroll=9)
    for b in range(count):
        sl = slice(b * 128, (b + 1) * 128)
        dq = heads_back(dq_s[b][:64]) * HEAD_DIM**-0.5
        dq_ref[sl, :] = full_turn(dq, cos_ref[sl, :], -sin_ref[sl, :]).astype(BF16)

    def unsort(tile, unused):
        for j in range(per):
            dkv_ref[slot[tile * per + j]] = acc_ref[tile, j * 128 : (j + 1) * 128, :].astype(BF16)
        return unused

    lax.fori_loop(0, acc_ref.shape[0], unsort, 0)


def attend_back(place, slot, me, rq, full, other, o, lse, ks, kt, cosine, sine, w_out):
    rows = rq.shape[0]
    width = w_out.shape[1]
    blocks = slot.shape[0]
    args = (rq, full, other, o, lse, ks, kt, cosine, sine)
    shapes = [
        jax.ShapeDtypeStruct(rq.shape, BF16),
        jax.ShapeDtypeStruct((blocks, 128, 128), BF16),
        jax.ShapeDtypeStruct((rows, width), BF16),
        jax.ShapeDtypeStruct((rows, 128), BF16),
    ]
    return pl.pallas_call(
        attend_back_kernel,
        grid_spec=pltpu.PrefetchScalarGridSpec(
            num_scalar_prefetch=3,
            grid=(1,),
            in_specs=[whole(a) for a in args]
            + [pl.BlockSpec((rq.shape[1], width), lambda i, place, slot, me: (me[0], 0))],
            out_specs=[whole(a) for a in shapes],
            scratch_shapes=[
                pltpu.VMEM(ks.shape, F32),
                pltpu.VMEM((rows // 128, 128, 512), BF16),
                pltpu.VMEM((rows // 128, 512, 128), BF16),
                pltpu.VMEM((rows // 128, 1, 256), F32),
                pltpu.VMEM((rows // 128, 128, 256), F32),
            ],
        ),
        out_shape=shapes,
        compiler_params=pltpu.CompilerParams(vmem_limit_bytes=LIMIT),
        cost_estimate=pl.CostEstimate(
            flops=30_000_000_000, bytes_accessed=8_000_000, transcendentals=4_000_000
        ),
        name="attend_back",
    )(place, slot, me, *args, w_out)


def whole(a):
    rank = len(a.shape)
    return pl.BlockSpec(a.shape, lambda i, *_: (0,) * rank, pipeline_mode=pl.Buffered(1))


def experts_kernel(
    me, o_ref, p_ref, x_ref, dy_ref, routes_ref, wo0, wo1, wo2, wo3, gain_ref, wr_ref,
    wg_ref, wu_ref, wd_ref,
    x2_ref, h2_ref, mix_ref, keep_ref, give_ref, mkeep_ref, mgive_ref, grad_ref,
    dh2_acc, moe_acc, dmix_acc, mix_s,
):
    step = pl.program_id(0)
    xh, core, first = me[1], me[2], me[3]
    rows = x_ref.shape[0]
    lane = lax.broadcasted_iota(jnp.int32, (rows, 128), 1)

    @pl.when(step == 0)
    def _():
        def heads(ref, side):
            return jnp.concatenate([ref[side], ref[2 + side]], 1)

        near = dot(heads(o_ref, xh), wo0[...]) + dot(heads(p_ref, xh), wo1[...])
        far = dot(heads(o_ref, 1 - xh), wo2[...]) + dot(heads(p_ref, 1 - xh), wo3[...])
        x2 = x_ref[...].astype(F32) + (near + far)
        few = rows // 8
        for j in range(8):

            @pl.when(me[4] == j)
            def _(j=j):
                x2_ref[...] = x2[j * few : (j + 1) * few]

        h2 = rms(x2, gain_ref[...])[0].astype(BF16)
        h2_ref[...] = h2
        logits = dot(h2, wr_ref[...])
        routes = routes_ref[...]
        used = lane == routes[:, 0:1]
        for k in range(1, routes.shape[1]):
            used = jnp.logical_or(used, lane == routes[:, k : k + 1])
        top = jnp.max(jnp.where(used, logits, -jnp.inf), 1, keepdims=True)
        expd = jnp.where(used, jnp.exp(logits - top), 0.0)
        mix_s[...] = expd / jnp.sum(expd, 1, keepdims=True)
        mix_ref[...] = mix_s[pl.ds(pl.multiple_of(me[4] * few, few), few), :]
        dh2_acc[...] = jnp.zeros_like(dh2_acc)
        moe_acc[...] = jnp.zeros_like(moe_acc)
        dmix_acc[...] = jnp.zeros_like(dmix_acc)

    here = lane == first + step
    gate = jnp.sum(jnp.where(here, mix_s[...], 0.0), 1, keepdims=True)
    h2 = h2_ref[...]
    dy = dy_ref[...].astype(F32)
    ga = dot(h2, wg_ref[0])
    up = dot(h2, wu_ref[0])
    sig = jax.nn.sigmoid(ga)
    act = ga * sig
    hid = (act * up).astype(BF16)
    eo = dot(hid, wd_ref[0])
    moe_acc[...] += gate * eo
    dmix_acc[...] += jnp.where(here, jnp.sum(dy * eo, 1, keepdims=True), 0.0)
    deo = (gate * dy).astype(BF16)
    dhid = inner(deo, wd_ref[0])
    dga = (dhid * up * (sig * (1.0 + ga * (1.0 - sig)))).astype(BF16)
    dup = (dhid * act).astype(BF16)
    dh2_acc[...] += inner(dga, wg_ref[0]) + inner(dup, wu_ref[0])
    groups = grad_ref.shape[0]
    across = grad_ref.shape[2] * 2 // 3
    width = h2.shape[1]
    grad_ref[:, 0, :across, :512] = outer(h2, dga).astype(BF16).reshape(groups, across, 512)
    grad_ref[:, 0, :across, 512:] = outer(h2, dup).astype(BF16).reshape(groups, across, 512)
    grad_ref[:, 0, across:, :] = outer(hid, deo).astype(BF16).reshape(groups, across // 2, width)

    @pl.when(step == pl.num_programs(0) - 1)
    def _():
        few = rows // 8
        for j in range(4):
            for side, out, mout in ((core, keep_ref, mkeep_ref), (1 - core, give_ref, mgive_ref)):
                at = pl.ds(pl.multiple_of((j * 2 + side) * few, few), few)
                out[j, :, :width] = dh2_acc[at, :].astype(BF16)
                out[j, :, width:] = dmix_acc[at, :].astype(BF16)
                mout[j] = moe_acc[at, :].astype(BF16)


def experts(me, o_mine, o_other, x_pair, dy_pair, routes, wo, gain, router, wg, wu, wd, groups):
    rows, width = x_pair.shape
    few = rows // 8
    local = wg.shape[0] // 2
    ff = wg.shape[2]
    args = (o_mine, o_other, x_pair, dy_pair, routes, *wo, gain, router)
    shapes = [
        jax.ShapeDtypeStruct((few, width), F32),
        jax.ShapeDtypeStruct((rows, width), BF16),
        jax.ShapeDtypeStruct((few, 128), F32),
        jax.ShapeDtypeStruct((4, few, width + 128), BF16),
        jax.ShapeDtypeStruct((4, few, width + 128), BF16),
        jax.ShapeDtypeStruct((4, few, width), BF16),
        jax.ShapeDtypeStruct((4, few, width), BF16),
    ]
    pick = lambda i, me: (me[0] * local + i, 0, 0)
    across = width // groups
    return pl.pallas_call(
        experts_kernel,
        grid_spec=pltpu.PrefetchScalarGridSpec(
            num_scalar_prefetch=1,
            grid=(local,),
            in_specs=[whole(a) for a in args]
            + [
                pl.BlockSpec((1, width, ff), pick),
                pl.BlockSpec((1, width, ff), pick),
                pl.BlockSpec((1, ff, width), pick),
            ],
            out_specs=[whole(a) for a in shapes]
            + [pl.BlockSpec((groups, 1, across * 3 // 2, width), lambda i, me: (0, i, 0, 0))],
            scratch_shapes=[
                pltpu.VMEM((rows, width), F32),
                pltpu.VMEM((rows, width), F32),
                pltpu.VMEM((rows, 128), F32),
                pltpu.VMEM((rows, 128), F32),
            ],
        ),
        out_shape=shapes
        + [jax.ShapeDtypeStruct((groups, local, across * 3 // 2, width), BF16)],
        compiler_params=pltpu.CompilerParams(vmem_limit_bytes=EXPERT_LIMIT),
        cost_estimate=pl.CostEstimate(
            flops=15_000_000_000, bytes_accessed=20_000_000, transcendentals=1_000_000
        ),
        name="experts",
    )(me, *args, wg, wu, wd)


def start_kernel(me, x_ref, gain_ref, wq_ref, wk_ref, wv_ref, cos_ref, sin_ref, keep_ref, give_ref):
    h1 = rms(x_ref[...].astype(F32), gain_ref[...])[0].astype(BF16)
    cosine, sine = cos_ref[...], sin_ref[...]
    query = full_turn(dot(h1, wq_ref[...]), cosine, sine)
    key = full_turn(dot(h1, wk_ref[...]), cosine, sine)
    value = dot(h1, wv_ref[...])
    left = lax.broadcasted_iota(jnp.int32, key.shape, 1) < 64
    halves = [
        jnp.concatenate([query[:, :128], jnp.where(left, key, pltpu.roll(value, 64, 1))], 1),
        jnp.concatenate([query[:, 128:], jnp.where(left, pltpu.roll(key, 64, 1), value)], 1),
    ]
    low = me[0] == 0
    keep_ref[...] = jnp.where(low, halves[0], halves[1]).astype(BF16)
    give_ref[...] = jnp.where(low, halves[1], halves[0]).astype(BF16)


def start(me, tokens, gain, wq, wk, wv, cosine, sine):
    args = (tokens, gain, wq, wk, wv, cosine, sine)
    shapes = [jax.ShapeDtypeStruct((tokens.shape[0], 256), BF16)] * 2
    return pl.pallas_call(
        start_kernel,
        grid_spec=pltpu.PrefetchScalarGridSpec(
            num_scalar_prefetch=1,
            grid=(1,),
            in_specs=[whole(a) for a in args],
            out_specs=[whole(a) for a in shapes],
        ),
        out_shape=shapes,
        compiler_params=pltpu.CompilerParams(vmem_limit_bytes=60 * 1024 * 1024),
        name="start",
    )(me, *args)


def middle_kernel(me, part_ref, x2_ref, mix_ref, dy_ref, gain_ref, wr_ref, out_ref):
    part = part_ref[0].astype(F32)
    for j in range(1, part_ref.shape[0]):
        part = part + part_ref[j].astype(F32)
    width = x2_ref.shape[1]
    mix, dmix = mix_ref[...], part[:, width:]
    dlogits = (mix * (dmix - jnp.sum(mix * dmix, 1, keepdims=True))).astype(BF16)
    dh2 = part[:, :width] + inner(dlogits, wr_ref[...])
    x2 = x2_ref[...]
    factor = lax.rsqrt(jnp.mean(x2 * x2, -1, keepdims=True) + EPS)
    scaled = dh2 * gain_ref[...]
    dx2 = dy_ref[...].astype(F32) + (
        factor * scaled - x2 * factor**3 * jnp.mean(scaled * x2, -1, keepdims=True)
    )
    gain = jnp.sum(dh2 * x2 * factor, 0, keepdims=True).astype(BF16).astype(F32)
    rows = x2.shape[0]
    per = width // rows
    at = lax.broadcasted_iota(jnp.int32, (rows, width), 1)
    spread = jnp.where(at // per == lax.broadcasted_iota(jnp.int32, (rows, width), 0), gain, 0.0)
    lane = lax.broadcasted_iota(jnp.int32, (width, 128), 1)
    place = lane == lax.broadcasted_iota(jnp.int32, (width, 128), 0) % per + 16
    extra = dot(spread.astype(BF16), place.astype(F32).astype(BF16)) + dlogits.astype(F32)
    for j in range(out_ref.shape[0]):
        out_ref[j, :, :width] = dx2.astype(BF16)
        out_ref[j, :, width:] = extra.astype(BF16)


def middle(me, part, x2, mix, dy, gain, router):
    few = part.shape[1]
    width = x2.shape[1]
    mine = lambda i, me: (me[4], 0)
    shape = jax.ShapeDtypeStruct(part.shape, BF16)
    return pl.pallas_call(
        middle_kernel,
        grid_spec=pltpu.PrefetchScalarGridSpec(
            num_scalar_prefetch=1,
            grid=(1,),
            in_specs=[
                whole(part),
                whole(x2),
                whole(mix),
                pl.BlockSpec((few, width), mine),
                whole(gain),
                whole(router),
            ],
            out_specs=whole(shape),
        ),
        out_shape=shape,
        compiler_params=pltpu.CompilerParams(vmem_limit_bytes=LIMIT),
        name="middle",
    )(me, part, x2, mix, dy, gain, router)


def collect_kernel(part_ref, cos_ref, sin_ref, out_ref):
    total = part_ref[0].astype(F32)
    for j in range(1, part_ref.shape[0]):
        total = total + part_ref[j].astype(F32)
    turned = full_turn(total, cos_ref[...], -sin_ref[...])
    left = lax.broadcasted_iota(jnp.int32, total.shape, 1) < 64
    out_ref[...] = jnp.where(left, turned, total).astype(BF16)


def collect(part, cosine, sine):
    shape = jax.ShapeDtypeStruct(part.shape[1:], BF16)
    args = (part, cosine, sine)
    return pl.pallas_call(
        collect_kernel,
        grid=(1,),
        in_specs=[whole(a) for a in args],
        out_specs=whole(shape),
        out_shape=shape,
        compiler_params=pltpu.CompilerParams(vmem_limit_bytes=LIMIT),
        name="collect",
    )(*args)


def finish_kernel(
    me, m_ref, o_ref, w0, w1, w2, w3, x_ref, gain_ref, da_ref,
    early_ref, gkv_ref, rest_ref, out_ref, small_ref,
):
    xh = me[1]

    def back(ref, side, w):
        one, two = ref[side], ref[2 + side]
        hq = one.shape[1] // 2
        left = lax.broadcasted_iota(jnp.int32, (one.shape[0], hq), 1) < 64
        low, high = one[:, hq:].astype(F32), two[:, hq:].astype(F32)
        keys = jnp.where(left, low, pltpu.roll(high, 64, 1)).astype(BF16)
        values = jnp.where(left, pltpu.roll(low, 64, 1), high).astype(BF16)
        return inner(jnp.concatenate([one[:, :hq], two[:, :hq], keys, values], 1), w[...])

    near = back(m_ref, xh, w0) + back(o_ref, xh, w1)
    far = back(m_ref, 1 - xh, w2) + back(o_ref, 1 - xh, w3)
    dh1 = near + far
    x = x_ref[...].astype(F32)
    factor = lax.rsqrt(jnp.mean(x * x, -1, keepdims=True) + EPS)
    scaled = dh1 * gain_ref[...]
    out_ref[...] = (
        da_ref[...].astype(F32)
        + factor * scaled
        - x * factor**3 * jnp.mean(scaled * x, -1, keepdims=True)
    ).astype(BF16)
    gain = jnp.sum(dh1 * x * factor, 0, keepdims=True)
    width = gain.shape[1]
    column = jnp.broadcast_to(gain, (128, width)).T
    lane = lax.broadcasted_iota(jnp.int32, (width, 128), 1)
    mark = rest_ref.shape[1] - 1
    small_ref[:, :256] = early_ref[...]
    small_ref[:, 256:384] = gkv_ref[...]
    small_ref[:, 384:] = jnp.where(lane == mark, column, rest_ref[...].astype(F32)).astype(BF16)


def finish(me, mine, other, ws, tokens, gain, da, early, gkv, rest):
    rows, width = tokens.shape
    args = (mine, other, *ws, tokens, gain)
    shapes = [
        jax.ShapeDtypeStruct((rows, width), BF16),
        jax.ShapeDtypeStruct((width, 512), BF16),
    ]
    return pl.pallas_call(
        finish_kernel,
        grid_spec=pltpu.PrefetchScalarGridSpec(
            num_scalar_prefetch=1,
            grid=(1,),
            in_specs=[whole(a) for a in args]
            + [pl.BlockSpec((rows, width), lambda i, me: (me[0], 0))]
            + [whole(a) for a in (early, gkv, rest)],
            out_specs=[whole(a) for a in shapes],
        ),
        out_shape=shapes,
        compiler_params=pltpu.CompilerParams(vmem_limit_bytes=LIMIT),
        name="finish",
    )(me, *args, da, early, gkv, rest)


def unpack_kernel(
    me, part_ref, keep_ref, got_ref, own_ref, near_ref, far_ref, last_ref,
    q_ref, k_ref, v_ref, o_ref, r_ref, nm_ref, na_ref, gate_ref, up_ref, down_ref, out_ref,
):
    local, few = keep_ref.shape[0], own_ref.shape[0]
    for ref, side in ((keep_ref, me[0]), (got_ref, 1 - me[0])):
        for e in range(local):
            gate_ref[side * local + e] = ref[e, : gate_ref.shape[1], : gate_ref.shape[2]].astype(F32)
            up_ref[side * local + e] = ref[e, : gate_ref.shape[1], gate_ref.shape[2] :].astype(F32)
            down_ref[side * local + e] = ref[e, gate_ref.shape[1] :, :].astype(F32)
    for ref, xh, core in (
        (own_ref, me[1], me[2]),
        (near_ref, me[1], 1 - me[2]),
        (far_ref, 1 - me[1], me[2]),
        (last_ref, 1 - me[1], 1 - me[2]),
    ):
        out_ref[pl.ds(pl.multiple_of((xh * 2 + core) * few, few), few), :] = ref[...]
    groups = part_ref.shape[0] // 2
    sums = []
    for side in (0, 1):
        total = part_ref[side].astype(F32)
        for j in range(1, groups):
            total = total + part_ref[2 * j + side].astype(F32)
        sums.append(total)
    one, two = sums
    q_ref[...] = jnp.concatenate([one[:, :128], two[:, :128]], 1)
    o_ref[...] = jnp.concatenate([one[:, 128:256], two[:, 128:256]], 1)
    left = lax.broadcasted_iota(jnp.int32, (one.shape[0], 128), 1) < 64
    low, high = one[:, 256:384], two[:, 256:384]
    k_ref[...] = jnp.where(left, low, pltpu.roll(high, 64, 1))
    v_ref[...] = jnp.where(left, pltpu.roll(low, 64, 1), high)
    rest = one[:, 384:] + two[:, 384:]
    rest = jnp.concatenate([rest, jnp.zeros((128 - rest.shape[0], 128), F32)], 0).T
    rows = q_ref.shape[0]
    count = r_ref.shape[0]
    r_ref[...] = rest[:count, :rows]
    nm_ref[...] = rest[count : count + 1, :rows]
    na_ref[...] = rest[127:, :rows]


def unpack(me, part, keep, got, outs, experts_all):
    rows = part.shape[1]
    local, width = keep.shape[0], keep.shape[2]
    args = (part, keep, got, *outs)
    shapes = [
        jax.ShapeDtypeStruct(n, F32)
        for n in (
            (rows, 256), (rows, 128), (rows, 128), (rows, 256), (experts_all, rows), (1, rows), (1, rows),
            (2 * local, rows, width // 2), (2 * local, rows, width // 2), (2 * local, rows // 2, width),
        )
    ] + [jax.ShapeDtypeStruct((4 * outs[0].shape[0], width), BF16)]
    return pl.pallas_call(
        unpack_kernel,
        grid_spec=pltpu.PrefetchScalarGridSpec(
            num_scalar_prefetch=1,
            grid=(1,),
            in_specs=[whole(a) for a in args],
            out_specs=[whole(a) for a in shapes],
        ),
        out_shape=shapes,
        compiler_params=pltpu.CompilerParams(vmem_limit_bytes=LIMIT),
        name="unpack",
    )(me, *args)


def on_device(
    tokens,
    cotangent,
    pairing,
    routes,
    norm_attn,
    w_query,
    w_key,
    w_value,
    w_out,
    norm_moe,
    w_router,
    w_gate,
    w_up,
    w_down,
):
    zy = lax.axis_index(ZY)
    xl = lax.axis_index("xl")
    wa = lax.axis_index(WA)
    rows, width = tokens.shape
    block = rows // 2
    both = 2 * rows
    count_ctx = pairing.shape[0]
    blocks = 2 * count_ctx
    groups = count_ctx // 2
    hq = w_query.shape[1] // 2
    hk = w_key.shape[1] // 2
    hall = hq + 2 * hk

    xh = lax.axis_index("xh")
    core = lax.axis_index("c")
    first = wa * w_gate.shape[0] + xl * (w_gate.shape[0] // 2)
    me = jnp.stack([xl, xh, core, first, xl * 4 + wa]).astype(jnp.int32)

    pair = lax.dynamic_slice_in_dim(pairing, zy * 2, 2)
    starts = jnp.stack([pair, blocks - 1 - pair], 1).reshape(4) * block
    qpos = (starts[:, None] + jnp.arange(block, dtype=jnp.int32)[None, :]).reshape(both)

    cos2, sin2 = lane_angles(qpos)
    own = lambda a: lax.dynamic_slice_in_dim(a, xl * rows, rows, 0)
    keep, give = start(
        me, tokens, norm_attn[None], w_query, w_key, w_value, own(cos2), own(sin2)
    )
    got = lax.ppermute(give, "xl", SWAP)
    low = xl == 0
    qkv = jnp.concatenate([jnp.where(low, keep, got), jnp.where(low, got, keep)], 0)
    rq = qkv[:, :hq]
    kv_mine = qkv[:, hq:]

    kv_all = lax.all_to_all(
        jnp.broadcast_to(kv_mine[None], (groups,) + kv_mine.shape), ZY, 0, 0, tiled=False
    ).reshape(blocks, block, 2 * hk)

    def ring_weights(w):
        near = lax.ppermute(w, "c", SWAP)
        far = lax.ppermute(w, "xh", SWAP)
        return w, near, far, lax.ppermute(far, "c", SWAP)

    w_outs = ring_weights(w_out)

    def ring_parts(w):
        return w, lax.ppermute(w, "c", SWAP), lax.ppermute(w, "xh", SWAP), lax.ppermute(
            w, WA, [(0, 3), (3, 0), (1, 2), (2, 1)]
        )

    x_pair = swap_x(tokens)
    routes_pair = swap_x(routes.astype(F32)).astype(jnp.int32)
    h1 = rms(x_pair.astype(F32), norm_attn)[0].astype(BF16)
    kv_all, x_pair, routes_pair, h1, cotangent = lax.optimization_barrier(
        (kv_all, x_pair, routes_pair, h1, cotangent)
    )
    dy_other = lax.ppermute(cotangent, "xl", SWAP)

    ranks = jnp.arange(count_ctx, dtype=jnp.int32)
    inverse = jnp.sum(jnp.where(pairing[None, :] == ranks[:, None], ranks[None, :], 0), 1)
    slot = jnp.concatenate([inverse * 2, inverse[::-1] * 2 + 1])
    place = starts // block
    attn_low, attn, lse, ks, kt = attend(place, slot, rq, kv_all)
    attn_low, dy_other, w_outs = lax.optimization_barrier((attn_low, dy_other, w_outs))
    dy_pair = in_pair(cotangent, dy_other)

    o_mine = lax.all_to_all(
        jnp.broadcast_to(attn_low[None], (4,) + attn_low.shape), CHIPS, 0, 0, tiled=False
    )
    w_in = jnp.concatenate([w_query, w_key, w_value], 1)
    o_mine, w_in, dy_pair = lax.optimization_barrier((o_mine, w_in, dy_pair))
    o_other = lax.ppermute(o_mine, "c", SWAP)
    experts_all = w_router.shape[1]
    router = jnp.pad(w_router, ((0, 0), (0, 128 - experts_all)))
    x2_rows, h2, mix_rows, keep, give, mkeep, mgive, grads = experts(
        me, o_mine, o_other, x_pair, dy_pair, routes_pair, w_outs, norm_moe[None], router,
        w_gate, w_up, w_down, groups,
    )

    def add(one, two):
        return (one.astype(F32) + two.astype(F32)).astype(BF16)

    part = add(keep, lax.ppermute(give, "c", SWAP))
    part = lax.all_to_all(part, CHIPS, 0, 0, tiled=False)
    grads = lax.psum_scatter(grads, "z", scatter_dimension=0, tiled=True)
    payload = middle(me, part, x2_rows, mix_rows, dy_pair, norm_moe[None], router)
    full = lax.all_to_all(payload, CHIPS, 0, 0, tiled=False)
    other = lax.ppermute(full, "c", SWAP)

    w_in, _ = lax.optimization_barrier((w_in, full))
    w_ins = ring_weights(w_in)
    dq, grad_kv, da, rest_pair = attend_back(
        place, slot, me, rq, full, other, attn, lse, ks, kt, cos2, sin2, w_out
    )
    mkeep, mgot, _ = lax.optimization_barrier(
        (mkeep, lax.ppermute(mgive, "c", SWAP), grad_kv)
    )
    moe = add(mkeep, mgot).reshape(2, 2, both // 8, width)
    at = lambda a, b: lax.dynamic_index_in_dim(
        lax.dynamic_index_in_dim(moe, a, 0, False), b, 0, False
    )
    few = both // 8
    moe_rows = (
        at(xl, xh).astype(F32)
        + lax.ppermute(at(1 - xl, xh), "xl", SWAP).astype(F32)
        + lax.ppermute(at(xl, 1 - xh), "xh", SWAP).astype(F32)
        + lax.ppermute(at(1 - xl, 1 - xh), CHIPS, [(0, 3), (3, 0), (1, 2), (2, 1)]).astype(F32)
    )
    out_rows = (x2_rows + moe_rows).astype(BF16)
    gnm_all = rest_pair[:, experts_all : experts_all + width // few].astype(F32)
    gnm_own = jnp.sum(own(gnm_all).reshape(4, few, width // few), 0).reshape(width)
    grad_kv = lax.all_to_all(
        grad_kv.reshape(groups, both, 2 * hk), ZY, 0, 0, tiled=False
    )
    h2_own = own(h2)
    rest = jnp.concatenate(
        [outer(h2_own, own(rest_pair)[:, :experts_all]), gnm_own[:, None]], 1
    ).astype(BF16)
    rest = jnp.pad(rest, ((0, 0), (0, 128 - rest.shape[1])))
    early = jnp.concatenate([outer(h1, dq), outer(da, attn_low)], 1).astype(BF16)
    outs = ring_parts(out_rows)
    grad_kv, rest, early, outs, w_ins, grads = lax.optimization_barrier(
        (grad_kv, rest, early, outs, w_ins, grads)
    )
    grads = lax.psum_scatter(grads, "y", scatter_dimension=0, tiled=True)[0]
    dkv = collect(grad_kv, cos2, sin2)

    def to_rows(piece):
        n = piece.shape[1]
        mine = lax.all_to_all(
            jnp.broadcast_to(piece.reshape(2, 1, rows, n), (2, 2, rows, n)).reshape(4, rows, n),
            CHIPS, 0, 0, tiled=False,
        )
        return mine, lax.ppermute(mine, "c", SWAP)

    d_mine, d_other = to_rows(jnp.concatenate([dq, dkv], 1))
    gkv = outer(h1, dkv).astype(BF16)
    grad_tokens, small = finish(
        me, d_mine, d_other, w_ins, tokens, norm_attn[None], da,
        early, gkv, rest,
    )

    local = grads.shape[0]
    nrow = width // groups // 2
    by_dest = jnp.concatenate(
        [
            grads[:, : 2 * nrow].reshape(local, 2, nrow, width),
            grads[:, 2 * nrow :].reshape(local, 2, nrow // 2, width),
        ],
        2,
    ).transpose(1, 0, 2, 3)
    by_dest, _ = lax.optimization_barrier((by_dest, small))
    keep_w = lax.dynamic_index_in_dim(by_dest, xl, 0, False)
    got_w = lax.ppermute(lax.dynamic_index_in_dim(by_dest, 1 - xl, 0, False), "xl", SWAP)

    small = lax.all_to_all(small.reshape(count_ctx, -1, small.shape[1]), CTX, 0, 0, tiled=False)
    (
        grad_query, grad_key, grad_value, grad_out, grad_router, gnm, gna, grad_gate, grad_up,
        grad_down, output,
    ) = unpack(me, small, keep_w, got_w, outs, experts_all)
    grad_out, grad_router = grad_out.T, grad_router.T
    grad_norm_moe, grad_norm_attn = gnm.reshape(-1), gna.reshape(-1)
    return (
        output,
        grad_tokens,
        grad_norm_attn,
        grad_query,
        grad_key,
        grad_value,
        grad_out,
        grad_norm_moe,
        grad_router,
        grad_gate,
        grad_up,
        grad_down,
    )


def solution(mesh):
    fine = Mesh(mesh.devices.reshape(4, 4, 2, 2, 2), ("z", "y", "xl", "xh", "c"))
    return jax.shard_map(
        on_device,
        mesh=fine,
        in_specs=(
            P(CTX, None),
            P(CTX, None),
            P(),
            P(CTX, None),
            P(),
            P(None, WA),
            P(None, WA),
            P(None, WA),
            P(WA, None),
            P(),
            P(),
            P(WA, None, None),
            P(WA, None, None),
            P(WA, None, None),
        ),
        out_specs=(
            P(CTX, None),
            P(CTX, None),
            P(CTX),
            P(CTX, WA),
            P(CTX, WA),
            P(CTX, WA),
            P(WA, CTX),
            P(CTX),
            P(CTX, None),
            P(WA, CTX, None),
            P(WA, CTX, None),
            P(WA, CTX, None),
        ),
        check_vma=False,
    )
```
